32 devices in a mesh: lat: 4 (over z), lon: 2 (over y), tm: 4 (over x, core).
Axes of the slice: x: 2, y: 2, z: 4, core: 2. Of those that a mesh axis runs over, the one named last changes fastest.
Arguments:
- signal: bfloat16 [4, 78, 32, 256], P('tm', None, 'lat', 'lon'), may hold values from -6 to 6
- dictionary: bfloat16 [64, 9984], P('lon'), may hold values from -0.0625 to 0.0625
- codes_init: float32 [4, 64, 8, 64], P('tm', None, 'lat', 'lon'), may hold values from -3 to 3
- thresholds: float32 [64], replicated, may hold values from 0.2 to 2
Outputs:
- codes: float32 [4, 64, 8, 64], P('tm', None, 'lat', 'lon')
- dict_grad: float32 [64, 9984], P('lon')
The draws below stay inside these ranges and needn't reach their ends.
All inputs are finite; a program needn't handle non-finite values.
Results may differ from the reference program's by a relative error of at most 0.0044.
Values may be sent and summed in bfloat16 or wider, within the bound.
A program may use at most 128 MiB of HBM per device.

```python
import math
import jax
import jax.numpy as jnp
from jax import lax

CHANNELS = 78
ATOMS = 64
ITERS = 2
ATOM_LEN = 9984
FRAMES = 4
HEIGHT = 32
WIDTH = 256
PZ = 8
QZ = 64


def shard_levels(key, extent, shards, least, high):
    level, own = 1.0, jax.random.fold_in(key, 6)
    for dim, shards_of in shards:
        heights = jnp.exp(jax.random.uniform(jax.random.fold_in(own, dim), (shards_of,), jnp.float32, least / len(shards), high / len(shards)))
        level = level * jnp.repeat(heights, extent[dim] // shards_of).reshape([-1 if axis == dim else 1 for axis in range(len(extent))])
    return level


def scatter_about(rng, extent, scale, limit, split=(), held_as=jnp.bfloat16):
    factor_of = shard_levels(rng, extent, split, -0.22, 0.18) if split else 1.0
    entries = jax.random.normal(rng, extent, jnp.float32) * scale * factor_of
    return jnp.minimum(jnp.maximum(entries, -limit), limit).astype(held_as)


def setup_inputs(seed: int = 0) -> dict:
    streams_of = jax.random.split(jax.random.key(seed), 5)
    return {
        "signal": scatter_about(streams_of[0], (FRAMES, CHANNELS, HEIGHT, WIDTH), 1.0, 6.0, ((0, 4), (2, 4), (3, 2))),
        "dictionary": scatter_about(streams_of[1], (ATOMS, ATOM_LEN), ATOM_LEN ** -0.5, 0.0625, ((0, 2),)),
        "codes_init": scatter_about(streams_of[2], (FRAMES, ATOMS, PZ, QZ), 0.5, 3.0, ((0, 4), (2, 4), (3, 2)), jnp.float32),
        "thresholds": jnp.clip(jnp.exp(jax.random.uniform(streams_of[3], (ATOMS,), jnp.float32, math.log(0.2), math.log(2.0))), 0.2, 2.0),
    }


STEP_SIZE = 0.5

def shift_codes(codes, delay, down, right):
    moved = jnp.roll(codes, right, axis=3)
    if down:
        moved = jnp.concatenate([jnp.zeros_like(moved[:, :, :1]), moved[:, :, :-1]], axis=2)
    if delay:
        moved = jnp.concatenate([jnp.zeros_like(moved[:, :1]), moved[:, :-1]], axis=1)
    return moved

def shift_back(resid, delay, down, right):
    moved = jnp.roll(resid, -right, axis=3)
    if down:
        moved = jnp.concatenate([moved[:, :, 1:], jnp.zeros_like(moved[:, :, :1])], axis=2)
    if delay:
        moved = jnp.concatenate([moved[:, 1:], jnp.zeros_like(moved[:, :1])], axis=1)
    return moved

def reference(signal, dictionary, codes_init, thresholds):
    frames, channels, height, width = signal.shape
    rows = height // 4
    columns = width // 4
    patch = channels * 16
    atoms = dictionary.shape[0]
    blocks = dictionary.reshape(atoms, 2, channels, 2, 4, 2, 4).transpose(1, 3, 5, 2, 4, 6, 0).reshape(8, patch, atoms)
    target = signal.reshape(frames, channels, rows, 4, columns, 4).transpose(1, 3, 5, 0, 2, 4)
    target = target.reshape(patch, frames, rows, columns)
    combos = [(delay, down, right) for delay in (0, 1) for down in (0, 1) for right in (0, 1)]

    def residual_of(current):
        coded = current.astype(jnp.bfloat16)
        total = jnp.zeros((patch, frames * rows * columns), jnp.float32)
        for index, (delay, down, right) in enumerate(combos):
            moved = shift_codes(coded, delay, down, right).reshape(atoms, -1)
            total = total + jnp.dot(blocks[index], moved, preferred_element_type=jnp.float32)
        return ((total.reshape(target.shape) - target).astype(jnp.bfloat16), coded)

    def adjoint(resid):
        total = jnp.zeros((atoms, frames * rows * columns), jnp.float32)
        for index, (delay, down, right) in enumerate(combos):
            moved = shift_back(resid, delay, down, right).reshape(patch, -1)
            total = total + lax.dot_general(blocks[index], moved, (((0,), (0,)), ((), ())), preferred_element_type=jnp.float32)
        return total.reshape(atoms, frames, rows, columns)
    current = jnp.transpose(codes_init, (1, 0, 2, 3))
    moving = current
    momentum_now = 1.0
    shrink = STEP_SIZE * thresholds[:, None, None, None]
    for turn in range(ITERS):
        resid, coded = residual_of(moving)
        descent = moving - STEP_SIZE * adjoint(resid)
        updated = jnp.sign(descent) * jnp.maximum(jnp.abs(descent) - shrink, 0.0)
        momentum_next = (1.0 + math.sqrt(1.0 + 4.0 * momentum_now * momentum_now)) / 2.0
        moving = updated + (momentum_now - 1.0) / momentum_next * (updated - current)
        current = updated
        momentum_now = momentum_next
    resid, coded = residual_of(current)
    flat_resid = resid.reshape(patch, -1)
    pieces = []
    for index, (delay, down, right) in enumerate(combos):
        moved = shift_codes(coded, delay, down, right).reshape(atoms, -1)
        pieces.append(lax.dot_general(flat_resid, moved, (((1,), (1,)), ((), ())), preferred_element_type=jnp.float32))
    grads = jnp.stack(pieces).reshape(2, 2, 2, channels, 4, 4, atoms).transpose(6, 0, 3, 1, 4, 2, 5)
    scale = 1.0 / math.sqrt(frames * rows * columns)
    dict_grad = grads.reshape(atoms, 2 * channels * 64) * scale
    return (jnp.transpose(current, (1, 0, 2, 3)), dict_grad)
```

```python
import functools
import math

import jax
import jax.numpy as jnp
import numpy as np
from jax import lax
from jax.experimental import pallas as pl
from jax.experimental.pallas import tpu as pltpu
from jax.sharding import PartitionSpec as P

ITERS = 2
STEP_SIZE = 0.5
MESH = pl.DeviceIdType.MESH
F32, BF16 = jnp.float32, jnp.bfloat16
COMBOS = [(h, a, b) for h in (0, 1) for a in (0, 1) for b in (0, 1)]
GROUP = 512


def cell_order():
    c, a, u, b, v = np.meshgrid(*[np.arange(n) for n in (8, 2, 4, 2, 4)], indexing="ij")
    source = ((((c * 2 + a) * 4 + u) * 2 + b) * 4 + v).ravel()
    target = ((((a * 2 + b) * 8 + c) * 4 + u) * 4 + v).ravel()
    order = np.zeros((GROUP, GROUP), np.float32)
    order[source, target] = 1.0
    return order


def contract(x, y, dx, dy):
    return lax.dot_general(x, y, (((dx,), (dy,)), ((), ())), preferred_element_type=F32)


def kernel(
    sizes, d_ref, p_ref, x_ref, z0_ref, th_ref, codes_ref, grad_ref,
    dfull, bhat, stage, zext, zs, cbuf, qbuf, acc, moving, current,
    gd, ra, sb, rb, sc, rc, sd, rd, fin,
    dict_s, dict_r, relay_s, relay_r, halo_s, halo_r, adj_s, adj_r,
    a_sem, b_s, b_r, c_sem, d_s, d_r, e_s, e_r, f_sem, g_sem,
):
    n_lat, n_lon, n_tm, atoms, rows, cols, half, padded = sizes
    owned = atoms // n_lon
    lat, lon, tm = lax.axis_index("lat"), lax.axis_index("lon"), lax.axis_index("tm")
    left = 8
    full = left + cols
    groups = padded // 128

    def at(la, lo, t):
        return (la, lo, t)

    def remote(src, dst, send, recv, where):
        return pltpu.make_async_remote_copy(
            src_ref=src, dst_ref=dst, send_sem=send, recv_sem=recv, device_id=where, device_id_type=MESH
        )

    def lon_at(step):
        return lax.rem(lon + step + n_lon, n_lon)

    zext[...] = jnp.zeros_like(zext)
    qbuf[...] = jnp.zeros_like(qbuf)

    def set_codes(turn, p, value):
        zext[turn, 0, 1 + p, left:full, :] = value.astype(BF16).astype(F32)

    for p in range(rows):
        value = z0_ref[p * cols : (p + 1) * cols, :]
        moving[p] = value
        current[p] = value
        set_codes(0, p, value)

    barrier = pltpu.get_barrier_semaphore()
    count = n_lat * n_lon * n_tm
    mine = (lat * n_lon + lon) * n_tm + tm

    def greet(step, carry):
        other = lax.rem(mine + step, count)
        where = (other // (n_lon * n_tm), lax.rem(other // n_tm, n_lon), lax.rem(other, n_tm))
        pl.semaphore_signal(barrier, inc=1, device_id=where, device_id_type=MESH)
        return carry

    lax.fori_loop(1, count, greet, 0)
    pl.semaphore_wait(barrier, count - 1)

    odd = lax.rem(tm, 2)
    upper = tm // 2
    pair = tm + 1 - 2 * odd
    cross = tm + 2 - 4 * upper

    def region(ref, head, da, dl, sender):
        r = (pl.ds(rows if sender else 0, 1)) if da else pl.ds(1, rows)
        c = (pl.ds(full - 8 if sender else 0, 8)) if dl else pl.ds(left, cols)
        return ref.at[head + (r, c)]

    def halo(turn, m):
        dt, da, dl = COMBOS[m]
        copy = remote(
            region(zext, (turn, 0), da, dl, True), region(zext, (turn, dt), da, dl, False),
            halo_s.at[turn, m], halo_r.at[turn, m],
            at(lax.rem(lat + da, n_lat), lon_at(dl), lax.rem(tm + dt, n_tm)),
        )
        sends = (tm + dt < n_tm) & (lat + da < n_lat)
        gets = (tm - dt >= 0) & (lat - da >= 0)
        return copy, sends, gets

    def adjoint(turn, m):
        dt, da, dl = COMBOS[m]
        copy = remote(
            region(cbuf, (turn, dt), da, dl, False), region(qbuf, (turn, dt), da, dl, False),
            adj_s.at[turn, m], adj_r.at[turn, m],
            at(lax.rem(lat - da + n_lat, n_lat), lon_at(-dl), lax.rem(tm - dt + n_tm, n_tm)),
        )
        sends = (tm - dt >= 0) & (lat - da >= 0)
        gets = (tm + dt < n_tm) & (lat + da < n_lat)
        return copy, sends, gets

    def start_all(make, turn):
        for m in range(1, 8):
            copy, sends, _ = make(turn, m)
            pl.when(sends)(copy.start)

    def wait_all(make, turn):
        for m in range(1, 8):
            copy, sends, gets = make(turn, m)
            pl.when(gets)(copy.wait_recv)
            pl.when(sends)(copy.wait_send)

    gathers = []
    for s in range(1, n_lon):
        copy = remote(
            d_ref.at[:, pl.ds(pl.multiple_of(odd * half, 128), half)], dfull.at[lon, odd],
            dict_s.at[s - 1], dict_r.at[s - 1], at(lat, lon_at(s), tm),
        )
        copy.start()
        gathers.append(copy)
    start_all(halo, 0)

    order = p_ref[...]

    def lay_out(load, place):
        for h in (0, 1):
            for g in range(groups):
                width = min(GROUP, half - g * GROUP)
                cells = jnp.dot(load(h, g * GROUP, width), order[:width], preferred_element_type=F32)
                for ab in range(4):
                    place((h * 4 + ab) * atoms, g * 128, cells[:, ab * 128 : (ab + 1) * 128])

    aligned = owned % 16 == 0

    def place_at(owner):
        def place(row, lane, value):
            if aligned:
                start = pl.multiple_of(row + owner * owned, 16)
                bhat[pl.ds(start, owned), lane : lane + 128] = value.astype(BF16)
            else:
                stage[row + owner * owned : row + owner * owned + owned, lane : lane + 128] = value
        return place

    if aligned:
        lay_out(lambda h, lane, width: d_ref[:, h * half + lane : h * half + lane + width], place_at(lon))
    relays = []
    for s in range(1, n_lon):
        source = lon_at(-s)
        gathers[s - 1].wait_recv()
        copy = remote(
            dfull.at[source, odd], dfull.at[source, odd], relay_s.at[s - 1], relay_r.at[s - 1], at(lat, lon, pair)
        )
        copy.start()
        relays.append(copy)
    for s in range(1, n_lon):
        source = lon_at(-s)
        relays[s - 1].wait_recv()
        if aligned:
            lay_out(lambda h, lane, width: dfull[source, h, :, lane : lane + width], place_at(source))
    if not aligned:
        for s in range(1, n_lon):
            gathers[s - 1].wait_send()
            relays[s - 1].wait_send()
        for h in (0, 1):
            dfull[lon, h] = d_ref[:, h * half : (h + 1) * half]
        for owner in range(n_lon):
            lay_out(lambda h, lane, width: dfull[owner, h, :, lane : lane + width], place_at(owner))
        bhat[...] = stage[...].astype(BF16)

    def stack_codes(turn):
        for i, (h, a, b) in enumerate(COMBOS):
            for p in range(rows):
                zs[p * cols : (p + 1) * cols, i * atoms : (i + 1) * atoms] = zext[
                    turn, h, 1 + p - a, left - b : full - b, :
                ]
        return zs[...].astype(BF16)

    def residual(stacked):
        synth = jnp.dot(stacked, bhat[...], preferred_element_type=F32)
        return (synth - x_ref[...].astype(F32)).astype(BF16)

    shrink = STEP_SIZE * th_ref[...]
    momentum = 1.0
    for turn in range(ITERS):
        wait_all(halo, turn)
        resid = residual(stack_codes(turn))
        terms = contract(resid, bhat[...], 1, 1)
        cbuf[turn] = jnp.zeros_like(cbuf[turn])
        for i, (h, a, b) in enumerate(COMBOS):
            for p in range(rows):
                cbuf[turn, h, 1 + p - a, left - b : full - b, :] += terms[
                    p * cols : (p + 1) * cols, i * atoms : (i + 1) * atoms
                ]
        start_all(adjoint, turn)
        wait_all(adjoint, turn)
        later = (1.0 + math.sqrt(1.0 + 4.0 * momentum * momentum)) / 2.0
        weight = (momentum - 1.0) / later
        momentum = later
        for p in range(rows):
            total = cbuf[turn, 0, 1 + p, left:full, :] + qbuf[turn, 1, 1 + p, left:full, :]
            edge = qbuf[turn, 0, 1 + p, 0:8, :] + qbuf[turn, 1, 1 + p, 0:8, :]
            if p == rows - 1:
                total = total + qbuf[turn, 0, 0, left:full, :] + qbuf[turn, 1, 0, left:full, :]
                edge = edge + qbuf[turn, 0, 0, 0:8, :] + qbuf[turn, 1, 0, 0:8, :]
            acc[...] = total
            acc[cols - 8 : cols, :] += edge
            descent = moving[p] - STEP_SIZE * acc[...]
            updated = jnp.where(
                descent > shrink, descent - shrink, jnp.where(descent < -shrink, descent + shrink, 0.0)
            )
            ahead = updated + weight * (updated - current[p])
            moving[p] = ahead
            current[p] = updated
            set_codes(turn + 1, p, ahead if turn < ITERS - 1 else updated)
        start_all(halo, turn + 1)
    for p in range(rows):
        codes_ref[p * cols : (p + 1) * cols, :] = current[p]
    wait_all(halo, ITERS)
    stacked = stack_codes(ITERS)
    resid = residual(stacked)

    for h in (0, 1):
        part = contract(stacked[:, h * 4 * atoms : (h + 1) * 4 * atoms], resid, 0, 0).astype(BF16)
        for g in range(groups):
            cells = jnp.concatenate(
                [part[ab * atoms : (ab + 1) * atoms, g * 128 : (g + 1) * 128] for ab in range(4)], axis=1
            )
            plain = contract(cells, order, 1, 1)
            for j in range(4):
                tile = 4 * g + j
                lane = tile % 5 * 128
                for owner in range(n_lon):
                    gd[h, tile // 5, owner, :, lane : lane + 128] = plain[
                        owner * owned : (owner + 1) * owned, j * 128 : (j + 1) * 128
                    ].astype(BF16)

    copy = remote(gd.at[1 - odd], ra, a_sem.at[0], a_sem.at[1], at(lat, lon, pair))
    copy.start()
    copy.wait()
    sb[...] = (gd[odd].astype(F32) + ra[...].astype(F32)).astype(BF16)
    copies = []
    for s in range(1, n_lon):
        copy = remote(sb.at[:, lon_at(s)], rb.at[s - 1], b_s.at[s - 1], b_r.at[s - 1], at(lat, lon_at(s), tm))
        copy.start()
        copies.append(copy)
    total = sb[:, lon].astype(F32)
    for s in range(1, n_lon):
        copies[s - 1].wait()
        total = total + rb[s - 1].astype(F32)
    sc[...] = total.astype(BF16)
    copy = remote(sc.at[pl.ds((1 - upper) * 4, 4)], rc, c_sem.at[0], c_sem.at[1], at(lat, lon, cross))
    copy.start()
    copy.wait()
    sd[...] = (sc[pl.ds(upper * 4, 4)].astype(F32) + rc[...].astype(F32)).astype(BF16)
    copies = []
    for s in range(1, n_lat):
        to = lax.rem(lat + s, n_lat)
        copy = remote(sd.at[to], rd.at[s - 1], d_s.at[s - 1], d_r.at[s - 1], at(to, lon, tm))
        copy.start()
        copies.append(copy)
    total = sd[lat].astype(F32)
    for s in range(1, n_lat):
        copies[s - 1].wait()
        total = total + rd[s - 1].astype(F32)
    eighth = upper * 4 + lat
    fin[odd, eighth] = total.astype(BF16)
    copies = []
    for s in range(1, n_lat):
        to = lax.rem(lat + s, n_lat)
        copy = remote(
            fin.at[odd, eighth], fin.at[odd, eighth], e_s.at[s - 1], e_r.at[s - 1], at(to, lon, tm)
        )
        copy.start()
        copies.append(copy)
    for copy in copies:
        copy.wait()
    four = fin.at[odd, pl.ds(upper * 4, 4)]
    copy = remote(four, four, f_sem.at[0], f_sem.at[1], at(lat, lon, cross))
    copy.start()
    copy.wait()
    copy = remote(fin.at[odd], fin.at[odd], g_sem.at[0], g_sem.at[1], at(lat, lon, pair))
    copy.start()
    copy.wait()
    for h in (0, 1):
        for eighth in range(8):
            width = min(640, half - eighth * 640)
            lane = h * half + eighth * 640
            grad_ref[:, lane : lane + width] = fin[h, eighth, :, :width]
    if aligned:
        for s in range(1, n_lon):
            gathers[s - 1].wait_send()
            relays[s - 1].wait_send()


def body(sizes, signal, dictionary, codes_init, thresholds):
    n_lat, n_lon, n_tm, atoms, rows, cols, half, padded = sizes
    channels = signal.shape[1]
    patch = channels * 16
    positions = rows * cols
    owned = dictionary.shape[0]
    target = signal[0].reshape(channels, rows, 4, cols, 4).transpose(1, 3, 0, 2, 4).reshape(positions, patch)
    target = jnp.pad(target, ((0, 0), (0, padded - patch)))
    start = codes_init[0].reshape(atoms, positions).T
    order = jnp.asarray(cell_order(), BF16)
    ext = (2, rows + 1, 8 + cols, atoms)
    dma = pltpu.SemaphoreType.DMA
    codes, grad = pl.pallas_call(
        functools.partial(kernel, sizes),
        out_shape=(
            jax.ShapeDtypeStruct((positions, atoms), F32),
            jax.ShapeDtypeStruct(dictionary.shape, BF16),
        ),
        in_specs=[pl.BlockSpec(memory_space=pltpu.VMEM)] * 5,
        out_specs=(pl.BlockSpec(memory_space=pltpu.VMEM),) * 2,
        scratch_shapes=[
            pltpu.VMEM((n_lon, 2, owned, half), BF16),
            pltpu.VMEM((8 * atoms, padded), BF16),
            pltpu.VMEM((8, 128) if owned % 16 == 0 else (8 * atoms, padded), F32),
            pltpu.VMEM((ITERS + 1,) + ext, F32),
            pltpu.VMEM((positions, 8 * atoms), F32),
            pltpu.VMEM((ITERS,) + ext, F32),
            pltpu.VMEM((ITERS,) + ext, F32),
            pltpu.VMEM((cols, atoms), F32),
            pltpu.VMEM((rows, cols, atoms), F32),
            pltpu.VMEM((rows, cols, atoms), F32),
            pltpu.VMEM((2, 8, n_lon, owned, 640), BF16),
            pltpu.VMEM((8, n_lon, owned, 640), BF16),
            pltpu.VMEM((8, n_lon, owned, 640), BF16),
            pltpu.VMEM((n_lon - 1, 8, owned, 640), BF16),
            pltpu.VMEM((8, owned, 640), BF16),
            pltpu.VMEM((4, owned, 640), BF16),
            pltpu.VMEM((4, owned, 640), BF16),
            pltpu.VMEM((n_lat - 1, owned, 640), BF16),
            pltpu.VMEM((2, 8, owned, 640), BF16),
            dma((n_lon - 1,)), dma((n_lon - 1,)), dma((n_lon - 1,)), dma((n_lon - 1,)),
            dma((ITERS + 1, 8)), dma((ITERS + 1, 8)), dma((ITERS, 8)), dma((ITERS, 8)),
            dma((2,)), dma((n_lon - 1,)), dma((n_lon - 1,)), dma((2,)),
            dma((n_lat - 1,)), dma((n_lat - 1,)), dma((n_lat - 1,)), dma((n_lat - 1,)),
            dma((2,)), dma((2,)),
        ],
        compiler_params=pltpu.CompilerParams(
            collective_id=0, has_side_effects=True, vmem_limit_bytes=48 * 2**20
        ),
        cost_estimate=pl.CostEstimate(flops=10**9, bytes_accessed=4 * 10**6, transcendentals=0),
    )(dictionary, order, target, start, thresholds[None, :])
    scale = 1.0 / math.sqrt(n_tm * n_lat * n_lon * positions)
    return codes.T.reshape(1, atoms, rows, cols), grad.astype(F32) * scale


def solution(mesh):
    n_lat, n_lon, n_tm = mesh.shape["lat"], mesh.shape["lon"], mesh.shape["tm"]
    assert n_lat == 4 and n_tm == 4 and n_lon >= 2
    placed = (P("tm", None, "lat", "lon"), P("lon", None), P("tm", None, "lat", "lon"), P())

    def part(signal, dictionary, codes_init, thresholds):
        atoms, rows, cols = codes_init.shape[1:]
        half = dictionary.shape[1] // 2
        sizes = (n_lat, n_lon, n_tm, atoms, rows, cols, half, -(-half // GROUP) * 128)
        return body(sizes, signal, dictionary, codes_init, thresholds)

    return jax.shard_map(
        part,
        mesh=mesh,
        in_specs=placed,
        out_specs=(P("tm", None, "lat", "lon"), P("lon", None)),
        check_vma=False,
    )
```

```python
import functools
import math

import jax
import jax.numpy as jnp
import numpy as np
from jax import lax
from jax.experimental import pallas as pl
from jax.experimental.pallas import tpu as pltpu
from jax.sharding import PartitionSpec as P

ITERS = 2
STEP_SIZE = 0.5
MESH = pl.DeviceIdType.MESH
F32, BF16 = jnp.float32, jnp.bfloat16
COMBOS = [(h, a, b) for h in (0, 1) for a in (0, 1) for b in (0, 1)]
GROUP = 512


def cell_order():
    c, a, u, b, v = np.meshgrid(*[np.arange(n) for n in (8, 2, 4, 2, 4)], indexing="ij")
    source = ((((c * 2 + a) * 4 + u) * 2 + b) * 4 + v).ravel()
    target = ((((a * 2 + b) * 8 + c) * 4 + u) * 4 + v).ravel()
    order = np.zeros((GROUP, GROUP), np.float32)
    order[source, target] = 1.0
    return order


def contract(x, y, dx, dy):
    return lax.dot_general(x, y, (((dx,), (dy,)), ((), ())), preferred_element_type=F32)


def kernel(
    sizes, d_ref, p_ref, x_ref, z0_ref, th_ref, codes_ref, grad_ref,
    dfull, bhat, stage, zext, zs, cbuf, qbuf, acc, moving, current,
    zh, away, home, ra, sb, rb, sc, rc, sd, rd, fin,
    dict_s, dict_r, relay_s, relay_r, halo_s, halo_r, adj_s, adj_r,
    a_s, a_r, b_s, b_r, c_s, c_r, d_s, d_r, e_s, e_r, f_s, f_r, g_s, g_r,
):
    n_lat, n_lon, n_tm, atoms, rows, cols, half, padded = sizes
    owned = atoms // n_lon
    lat, lon, tm = lax.axis_index("lat"), lax.axis_index("lon"), lax.axis_index("tm")
    left = 8
    full = left + cols
    groups = padded // 128

    def at(la, lo, t):
        return (la, lo, t)

    def remote(src, dst, send, recv, where):
        return pltpu.make_async_remote_copy(
            src_ref=src, dst_ref=dst, send_sem=send, recv_sem=recv, device_id=where, device_id_type=MESH
        )

    def lon_at(step):
        return lax.rem(lon + step + n_lon, n_lon)

    zext[...] = jnp.zeros_like(zext)
    qbuf[...] = jnp.zeros_like(qbuf)

    def set_codes(turn, p, value):
        zext[turn, 0, 1 + p, left:full, :] = value.astype(BF16).astype(F32)

    for p in range(rows):
        value = z0_ref[p * cols : (p + 1) * cols, :]
        moving[p] = value
        current[p] = value
        set_codes(0, p, value)

    barrier = pltpu.get_barrier_semaphore()
    count = n_lat * n_lon * n_tm
    mine = (lat * n_lon + lon) * n_tm + tm

    def greet(step, carry):
        other = lax.rem(mine + step, count)
        where = (other // (n_lon * n_tm), lax.rem(other // n_tm, n_lon), lax.rem(other, n_tm))
        pl.semaphore_signal(barrier, inc=1, device_id=where, device_id_type=MESH)
        return carry

    lax.fori_loop(1, count, greet, 0)
    pl.semaphore_wait(barrier, count - 1)

    odd = lax.rem(tm, 2)
    upper = tm // 2
    pair = tm + 1 - 2 * odd
    cross = tm + 2 - 4 * upper

    def region(ref, head, da, dl, sender):
        r = (pl.ds(rows if sender else 0, 1)) if da else pl.ds(1, rows)
        c = (pl.ds(full - 8 if sender else 0, 8)) if dl else pl.ds(left, cols)
        return ref.at[head + (r, c)]

    def halo(turn, m):
        dt, da, dl = COMBOS[m]
        copy = remote(
            region(zext, (turn, 0), da, dl, True), region(zext, (turn, dt), da, dl, False),
            halo_s.at[turn, m], halo_r.at[turn, m],
            at(lax.rem(lat + da, n_lat), lon_at(dl), lax.rem(tm + dt, n_tm)),
        )
        sends = (tm + dt < n_tm) & (lat + da < n_lat)
        gets = (tm - dt >= 0) & (lat - da >= 0)
        return copy, sends, gets

    def adjoint(turn, m):
        dt, da, dl = COMBOS[m]
        copy = remote(
            region(cbuf, (turn, dt), da, dl, False), region(qbuf, (turn, dt), da, dl, False),
            adj_s.at[turn, m], adj_r.at[turn, m],
            at(lax.rem(lat - da + n_lat, n_lat), lon_at(-dl), lax.rem(tm - dt + n_tm, n_tm)),
        )
        sends = (tm - dt >= 0) & (lat - da >= 0)
        gets = (tm + dt < n_tm) & (lat + da < n_lat)
        return copy, sends, gets

    def start_all(make, turn):
        for m in range(1, 8):
            copy, sends, _ = make(turn, m)
            pl.when(sends)(copy.start)

    def wait_all(make, turn):
        for m in range(1, 8):
            copy, sends, gets = make(turn, m)
            pl.when(gets)(copy.wait_recv)
            pl.when(sends)(copy.wait_send)

    lanes = [(g, min(g + 4, groups)) for g in range(0, groups, 4)]
    spans = [(g0 * GROUP, min(g1 * GROUP, half)) for g0, g1 in lanes]
    gathers = {}
    for c, (first, last) in enumerate(spans):
        for s in range(1, n_lon):
            copy = remote(
                d_ref.at[:, pl.ds(pl.multiple_of(odd * half + first, 128), last - first)],
                dfull.at[lon, odd, :, pl.ds(first, last - first)],
                dict_s.at[c, s - 1], dict_r.at[c, s - 1], at(lat, lon_at(s), tm),
            )
            copy.start()
            gathers[c, s] = copy
        if c == 0:
            start_all(halo, 0)

    order = p_ref[...]

    def lay_out(load, place, chunk):
        g0, g1 = lanes[chunk]
        pieces = []
        for g in range(g0, g1):
            width = min(GROUP, half - g * GROUP)
            piece = load(g * GROUP, width)
            if width < GROUP:
                piece = jnp.concatenate([piece, jnp.zeros((owned, GROUP - width), BF16)], axis=1)
            pieces.append(piece)
        cells = jnp.dot(jnp.concatenate(pieces, axis=0), order, preferred_element_type=F32)
        for g in range(g0, g1):
            for ab in range(4):
                place(ab * atoms, g * 128, cells[(g - g0) * owned : (g - g0 + 1) * owned, ab * 128 : (ab + 1) * 128])

    aligned = owned % 16 == 0

    def place_at(owner, h):
        def place(row, lane, value):
            if aligned:
                start = pl.multiple_of(h * 4 * atoms + row + owner * owned, 16)
                bhat[pl.ds(start, owned), lane : lane + 128] = value.astype(BF16)
            else:
                start = h * 4 * atoms + row + owner * owned
                stage[start : start + owned, lane : lane + 128] = value
        return place

    def lay_out_small(owner, h, chunk):
        for g in range(*lanes[chunk]):
            width = min(GROUP, half - g * GROUP)
            cells = jnp.dot(held(owner, h)(g * GROUP, width), order[:width], preferred_element_type=F32)
            for ab in range(4):
                place_at(owner, h)(ab * atoms, g * 128, cells[:, ab * 128 : (ab + 1) * 128])

    def held(owner, h):
        return lambda lane, width: dfull[owner, h, :, lane : lane + width]

    if aligned:
        for c in range(len(lanes)):
            for h in (0, 1):
                lay_out(
                    lambda lane, width: d_ref[:, h * half + lane : h * half + lane + width], place_at(lon, h), c
                )
    relays = {}

    def relayed(c):
        for s in range(1, n_lon):
            source = lon_at(-s)
            relays[c, s].wait_recv()
            if aligned:
                lay_out(held(source, 1 - odd), place_at(source, 1 - odd), c)

    for c, (first, last) in enumerate(spans):
        for s in range(1, n_lon):
            source = lon_at(-s)
            gathers[c, s].wait_recv()
            part = dfull.at[source, odd, :, pl.ds(first, last - first)]
            copy = remote(part, part, relay_s.at[c, s - 1], relay_r.at[c, s - 1], at(lat, lon, pair))
            copy.start()
            relays[c, s] = copy
            if aligned:
                lay_out(held(source, odd), place_at(source, odd), c)
        if c > 0:
            relayed(c - 1)
    relayed(len(lanes) - 1)
    if not aligned:
        for copy in [*gathers.values(), *relays.values()]:
            copy.wait_send()
        for h in (0, 1):
            dfull[lon, h] = d_ref[:, h * half : (h + 1) * half]
            for c in range(len(lanes)):
                for owner in range(n_lon):
                    lay_out_small(owner, h, c)
        bhat[...] = stage[...].astype(BF16)

    def stack_codes(turn):
        for i, (h, a, b) in enumerate(COMBOS):
            for p in range(rows):
                zs[p * cols : (p + 1) * cols, i * atoms : (i + 1) * atoms] = zext[
                    turn, h, 1 + p - a, left - b : full - b, :
                ]
        return zs[...].astype(BF16)

    def residual(stacked):
        synth = jnp.dot(stacked, bhat[...], preferred_element_type=F32)
        return (synth - x_ref[...].astype(F32)).astype(BF16)

    shrink = STEP_SIZE * th_ref[...]
    momentum = 1.0
    for turn in range(ITERS):
        wait_all(halo, turn)
        resid = residual(stack_codes(turn))
        terms = contract(resid, bhat[...], 1, 1)
        cbuf[turn] = jnp.zeros_like(cbuf[turn])
        for i, (h, a, b) in enumerate(COMBOS):
            for p in range(rows):
                cbuf[turn, h, 1 + p - a, left - b : full - b, :] += terms[
                    p * cols : (p + 1) * cols, i * atoms : (i + 1) * atoms
                ]
        start_all(adjoint, turn)
        wait_all(adjoint, turn)
        later = (1.0 + math.sqrt(1.0 + 4.0 * momentum * momentum)) / 2.0
        weight = (momentum - 1.0) / later
        momentum = later
        for p in range(rows):
            total = cbuf[turn, 0, 1 + p, left:full, :] + qbuf[turn, 1, 1 + p, left:full, :]
            edge = qbuf[turn, 0, 1 + p, 0:8, :] + qbuf[turn, 1, 1 + p, 0:8, :]
            if p == rows - 1:
                total = total + qbuf[turn, 0, 0, left:full, :] + qbuf[turn, 1, 0, left:full, :]
                edge = edge + qbuf[turn, 0, 0, 0:8, :] + qbuf[turn, 1, 0, 0:8, :]
            acc[...] = total
            acc[cols - 8 : cols, :] += edge
            descent = moving[p] - STEP_SIZE * acc[...]
            updated = jnp.where(
                descent > shrink, descent - shrink, jnp.where(descent < -shrink, descent + shrink, 0.0)
            )
            ahead = updated + weight * (updated - current[p])
            moving[p] = ahead
            current[p] = updated
            set_codes(turn + 1, p, ahead if turn < ITERS - 1 else updated)
        start_all(halo, turn + 1)
    for p in range(rows):
        codes_ref[p * cols : (p + 1) * cols, :] = current[p]
    wait_all(halo, ITERS)
    stacked = stack_codes(ITERS)
    resid = residual(stacked)

    wide = 4 * atoms
    chunks = groups // 2
    for h in (0, 1):
        zh[h] = stacked[:, h * wide : (h + 1) * wide]
    part_of = [resid[:, j * 256 : (j + 1) * 256] for j in range(chunks)]
    pairs = []
    for j in range(chunks):
        away[j] = contract(zh[1 - odd], part_of[j], 0, 0)
        copy = remote(away.at[j], ra.at[j], a_s.at[j], a_r.at[j], at(lat, lon, pair))
        copy.start()
        pairs.append(copy)
    for j in range(chunks):
        home[j] = contract(zh[odd], part_of[j], 0, 0)
    eighth = upper * 4 + lat

    def lon_stage(j):
        pairs[j].wait()
        part = (home[j] + ra[j]).astype(BF16)
        cells = jnp.concatenate(
            [
                jnp.concatenate(
                    [part[ab * atoms : (ab + 1) * atoms, g * 128 : (g + 1) * 128] for ab in range(4)], axis=1
                )
                for g in (0, 1)
            ],
            axis=0,
        )
        plain = contract(cells, order, 1, 1)
        for tile in range(8):
            row, lane = tile // 4 * atoms, tile % 4 * 128
            for owner in range(n_lon):
                sb[j, tile, owner] = plain[
                    row + owner * owned : row + (owner + 1) * owned, lane : lane + 128
                ].astype(BF16)
        return [
            remote(
                sb.at[j, :, lon_at(s)], rb.at[s - 1, j], b_s.at[j, s - 1], b_r.at[j, s - 1], at(lat, lon_at(s), tm)
            )
            for s in range(1, n_lon)
        ]

    def cross_stage(j):
        total = sb[j, :, lon].astype(F32)
        for s in range(1, n_lon):
            total = total + rb[s - 1, j].astype(F32)
        sc[j] = total.astype(BF16)
        return [
            remote(sc.at[j, pl.ds((1 - upper) * 4, 4)], rc.at[j], c_s.at[j], c_r.at[j], at(lat, lon, cross))
        ]

    def lat_stage(j):
        sd[j] = (sc[j, pl.ds(upper * 4, 4)].astype(F32) + rc[j].astype(F32)).astype(BF16)
        copies = []
        for s in range(1, n_lat):
            to = lax.rem(lat + s, n_lat)
            copies.append(
                remote(sd.at[j, to], rd.at[s - 1, j], d_s.at[j, s - 1], d_r.at[j, s - 1], at(to, lon, tm))
            )
        return copies

    def lat_back(j):
        total = sd[j, lat].astype(F32)
        for s in range(1, n_lat):
            total = total + rd[s - 1, j].astype(F32)
        fin[odd, j, eighth] = total.astype(BF16)
        own = fin.at[odd, j, eighth]
        return [
            remote(own, own, e_s.at[j, s - 1], e_r.at[j, s - 1], at(lax.rem(lat + s, n_lat), lon, tm))
            for s in range(1, n_lat)
        ]

    def cross_back(j):
        own = fin.at[odd, j, pl.ds(upper * 4, 4)]
        return [remote(own, own, f_s.at[j], f_r.at[j], at(lat, lon, cross))]

    def pair_back(j):
        own = fin.at[odd, j]
        return [remote(own, own, g_s.at[j], g_r.at[j], at(lat, lon, pair))]

    def finish(j):
        for h in (0, 1):
            for tile in range(8):
                lane = (8 * j + tile) * 128
                if lane < half:
                    grad_ref[:, h * half + lane : h * half + lane + 128] = fin[h, j, tile]
        return []

    stages = [lon_stage, cross_stage, lat_stage, lat_back, cross_back, pair_back, finish]
    flying = {}
    for step in range(chunks + len(stages) - 1):
        for number in reversed(range(len(stages))):
            j = step - number
            if 0 <= j < chunks:
                for copy in flying.get(j, []):
                    copy.wait()
                flying[j] = stages[number](j)
                for copy in flying[j]:
                    copy.start()
    if aligned:
        for copy in [*gathers.values(), *relays.values()]:
            copy.wait_send()


def body(sizes, signal, dictionary, codes_init, thresholds):
    n_lat, n_lon, n_tm, atoms, rows, cols, half, padded = sizes
    channels = signal.shape[1]
    patch = channels * 16
    positions = rows * cols
    owned = dictionary.shape[0]
    target = signal[0].reshape(channels, rows, 4, cols, 4).transpose(1, 3, 0, 2, 4).reshape(positions, patch)
    target = jnp.pad(target, ((0, 0), (0, padded - patch)))
    start = codes_init[0].reshape(atoms, positions).T
    order = jnp.asarray(cell_order(), BF16)
    ext = (2, rows + 1, 8 + cols, atoms)
    dma = pltpu.SemaphoreType.DMA
    chunks, spans = padded // 256, -(-padded // 512)
    codes, grad = pl.pallas_call(
        functools.partial(kernel, sizes),
        out_shape=(
            jax.ShapeDtypeStruct((positions, atoms), F32),
            jax.ShapeDtypeStruct(dictionary.shape, BF16),
        ),
        in_specs=[pl.BlockSpec(memory_space=pltpu.VMEM)] * 5,
        out_specs=(pl.BlockSpec(memory_space=pltpu.VMEM),) * 2,
        scratch_shapes=[
            pltpu.VMEM((n_lon, 2, owned, half), BF16),
            pltpu.VMEM((8 * atoms, padded), BF16),
            pltpu.VMEM((8, 128) if owned % 16 == 0 else (8 * atoms, padded), F32),
            pltpu.VMEM((ITERS + 1,) + ext, F32),
            pltpu.VMEM((positions, 8 * atoms), F32),
            pltpu.VMEM((ITERS,) + ext, F32),
            pltpu.VMEM((ITERS,) + ext, F32),
            pltpu.VMEM((cols, atoms), F32),
            pltpu.VMEM((rows, cols, atoms), F32),
            pltpu.VMEM((rows, cols, atoms), F32),
            pltpu.VMEM((2, positions, 4 * atoms), BF16),
            pltpu.VMEM((chunks, 4 * atoms, 256), F32),
            pltpu.VMEM((chunks, 4 * atoms, 256), F32),
            pltpu.VMEM((chunks, 4 * atoms, 256), F32),
            pltpu.VMEM((chunks, 8, n_lon, owned, 128), BF16),
            pltpu.VMEM((n_lon - 1, chunks, 8, owned, 128), BF16),
            pltpu.VMEM((chunks, 8, owned, 128), BF16),
            pltpu.VMEM((chunks, 4, owned, 128), BF16),
            pltpu.VMEM((chunks, 4, owned, 128), BF16),
            pltpu.VMEM((n_lat - 1, chunks, owned, 128), BF16),
            pltpu.VMEM((2, chunks, 8, owned, 128), BF16),
            dma((spans, n_lon - 1)), dma((spans, n_lon - 1)), dma((spans, n_lon - 1)), dma((spans, n_lon - 1)),
            dma((ITERS + 1, 8)), dma((ITERS + 1, 8)), dma((ITERS, 8)), dma((ITERS, 8)),
            dma((chunks,)), dma((chunks,)), dma((chunks, n_lon - 1)), dma((chunks, n_lon - 1)),
            dma((chunks,)), dma((chunks,)),
            dma((chunks, n_lat - 1)), dma((chunks, n_lat - 1)), dma((chunks, n_lat - 1)), dma((chunks, n_lat - 1)),
            dma((chunks,)), dma((chunks,)), dma((chunks,)), dma((chunks,)),
        ],
        compiler_params=pltpu.CompilerParams(
            collective_id=0, has_side_effects=True, vmem_limit_bytes=48 * 2**20
        ),
        cost_estimate=pl.CostEstimate(flops=10**9, bytes_accessed=4 * 10**6, transcendentals=0),
    )(dictionary, order, target, start, thresholds[None, :])
    scale = 1.0 / math.sqrt(n_tm * n_lat * n_lon * positions)
    return codes.T.reshape(1, atoms, rows, cols), grad.astype(F32) * scale


def solution(mesh):
    n_lat, n_lon, n_tm = mesh.shape["lat"], mesh.shape["lon"], mesh.shape["tm"]
    assert n_lat == 4 and n_tm == 4 and n_lon >= 2
    placed = (P("tm", None, "lat", "lon"), P("lon", None), P("tm", None, "lat", "lon"), P())

    def part(signal, dictionary, codes_init, thresholds):
        atoms, rows, cols = codes_init.shape[1:]
        half = dictionary.shape[1] // 2
        sizes = (n_lat, n_lon, n_tm, atoms, rows, cols, half, -(-half // GROUP) * 128)
        return body(sizes, signal, dictionary, codes_init, thresholds)

    return jax.shard_map(
        part,
        mesh=mesh,
        in_specs=placed,
        out_specs=(P("tm", None, "lat", "lon"), P("lon", None)),
        check_vma=False,
    )
```

```python
import functools
import math

import jax
import jax.numpy as jnp
import numpy as np
from jax import lax
from jax.experimental import pallas as pl
from jax.experimental.pallas import tpu as pltpu
from jax.sharding import PartitionSpec as P

ITERS = 2
STEP_SIZE = 0.5
MESH = pl.DeviceIdType.MESH
F32, BF16 = jnp.float32, jnp.bfloat16
COMBOS = [(h, a, b) for h in (0, 1) for a in (0, 1) for b in (0, 1)]
GROUP = 512


def cell_order():
    c, a, u, b, v = np.meshgrid(*[np.arange(n) for n in (8, 2, 4, 2, 4)], indexing="ij")
    source = ((((c * 2 + a) * 4 + u) * 2 + b) * 4 + v).ravel()
    target = ((((a * 2 + b) * 8 + c) * 4 + u) * 4 + v).ravel()
    order = np.zeros((GROUP, GROUP), np.float32)
    order[source, target] = 1.0
    return order


def contract(x, y, dx, dy):
    return lax.dot_general(x, y, (((dx,), (dy,)), ((), ())), preferred_element_type=F32)


def kernel(
    sizes, d_ref, p_ref, x_ref, z0_ref, th_ref, codes_ref, grad_ref,
    dfull, bhat, stage, zext, zs, cbuf, qbuf, acc, moving, current,
    zh, away, home, ra, sb, rb, sc, rc, sd, rd, fin,
    dict_s, dict_r, relay_s, relay_r, halo_s, halo_r, adj_s, adj_r,
    a_s, a_r, b_s, b_r, c_s, c_r, d_s, d_r, e_s, e_r, f_s, f_r, g_s, g_r,
):
    n_lat, n_lon, n_tm, atoms, rows, cols, half, padded = sizes
    owned = atoms // n_lon
    lat, lon, tm = lax.axis_index("lat"), lax.axis_index("lon"), lax.axis_index("tm")
    left = 8
    full = left + cols
    groups = padded // 128

    def at(la, lo, t):
        return (la, lo, t)

    def remote(src, dst, send, recv, where):
        return pltpu.make_async_remote_copy(
            src_ref=src, dst_ref=dst, send_sem=send, recv_sem=recv, device_id=where, device_id_type=MESH
        )

    def lon_at(step):
        return lax.rem(lon + step + n_lon, n_lon)

    zext[...] = jnp.zeros_like(zext)
    qbuf[...] = jnp.zeros_like(qbuf)

    def set_codes(turn, p, value):
        zext[turn, 0, 1 + p, left:full, :] = value.astype(BF16).astype(F32)

    for p in range(rows):
        value = z0_ref[p * cols : (p + 1) * cols, :]
        moving[p] = value
        current[p] = value
        set_codes(0, p, value)

    barrier = pltpu.get_barrier_semaphore()
    count = n_lat * n_lon * n_tm
    mine = (lat * n_lon + lon) * n_tm + tm

    def greet(step, carry):
        other = lax.rem(mine + step, count)
        where = (other // (n_lon * n_tm), lax.rem(other // n_tm, n_lon), lax.rem(other, n_tm))
        pl.semaphore_signal(barrier, inc=1, device_id=where, device_id_type=MESH)
        return carry

    lax.fori_loop(1, count, greet, 0)
    pl.semaphore_wait(barrier, count - 1)

    odd = lax.rem(tm, 2)
    upper = tm // 2
    pair = tm + 1 - 2 * odd
    cross = tm + 2 - 4 * upper

    def region(ref, head, da, dl, sender):
        r = (pl.ds(rows if sender else 0, 1)) if da else pl.ds(1, rows)
        c = (pl.ds(full - 8 if sender else 0, 8)) if dl else pl.ds(left, cols)
        return ref.at[head + (r, c)]

    def halo(turn, m):
        dt, da, dl = COMBOS[m]
        copy = remote(
            region(zext, (turn, 0), da, dl, True), region(zext, (turn, dt), da, dl, False),
            halo_s.at[turn, m], halo_r.at[turn, m],
            at(lax.rem(lat + da, n_lat), lon_at(dl), lax.rem(tm + dt, n_tm)),
        )
        sends = (tm + dt < n_tm) & (lat + da < n_lat)
        gets = (tm - dt >= 0) & (lat - da >= 0)
        return copy, sends, gets

    def adjoint(turn, m):
        dt, da, dl = COMBOS[m]
        copy = remote(
            region(cbuf, (turn, dt), da, dl, False), region(qbuf, (turn, dt), da, dl, False),
            adj_s.at[turn, m], adj_r.at[turn, m],
            at(lax.rem(lat - da + n_lat, n_lat), lon_at(-dl), lax.rem(tm - dt + n_tm, n_tm)),
        )
        sends = (tm - dt >= 0) & (lat - da >= 0)
        gets = (tm + dt < n_tm) & (lat + da < n_lat)
        return copy, sends, gets

    def start_all(make, turn):
        for m in range(1, 8):
            copy, sends, _ = make(turn, m)
            pl.when(sends)(copy.start)

    def wait_all(make, turn):
        for m in range(1, 8):
            copy, sends, gets = make(turn, m)
            pl.when(gets)(copy.wait_recv)
            pl.when(sends)(copy.wait_send)

    lanes = [(g, min(g + 4, groups)) for g in range(0, groups, 4)]
    spans = [(g0 * GROUP, min(g1 * GROUP, half)) for g0, g1 in lanes]
    gathers = {}
    for c, (first, last) in enumerate(spans):
        for s in range(1, n_lon):
            copy = remote(
                d_ref.at[:, pl.ds(pl.multiple_of(odd * half + first, 128), last - first)],
                dfull.at[lon, odd, :, pl.ds(first, last - first)],
                dict_s.at[c, s - 1], dict_r.at[c, s - 1], at(lat, lon_at(s), tm),
            )
            copy.start()
            gathers[c, s] = copy
        if c == 0:
            start_all(halo, 0)

    order = p_ref[...]

    def lay_out(load, place, chunk):
        g0, g1 = lanes[chunk]
        pieces = []
        for g in range(g0, g1):
            width = min(GROUP, half - g * GROUP)
            piece = load(g * GROUP, width)
            if width < GROUP:
                piece = jnp.concatenate([piece, jnp.zeros((owned, GROUP - width), BF16)], axis=1)
            pieces.append(piece)
        cells = jnp.dot(jnp.concatenate(pieces, axis=0), order, preferred_element_type=F32)
        for g in range(g0, g1):
            for ab in range(4):
                place(ab * atoms, g * 128, cells[(g - g0) * owned : (g - g0 + 1) * owned, ab * 128 : (ab + 1) * 128])

    aligned = owned % 16 == 0

    def place_at(owner, h):
        def place(row, lane, value):
            if aligned:
                start = pl.multiple_of(h * 4 * atoms + row + owner * owned, 16)
                bhat[pl.ds(start, owned), lane : lane + 128] = value.astype(BF16)
            else:
                start = h * 4 * atoms + row + owner * owned
                stage[start : start + owned, lane : lane + 128] = value
        return place

    def lay_out_small(owner, h, chunk):
        for g in range(*lanes[chunk]):
            width = min(GROUP, half - g * GROUP)
            cells = jnp.dot(held(owner, h)(g * GROUP, width), order[:width], preferred_element_type=F32)
            for ab in range(4):
                place_at(owner, h)(ab * atoms, g * 128, cells[:, ab * 128 : (ab + 1) * 128])

    def held(owner, h):
        return lambda lane, width: dfull[owner, h, :, lane : lane + width]

    if aligned:
        for c in range(len(lanes)):
            for h in (0, 1):
                lay_out(
                    lambda lane, width: d_ref[:, h * half + lane : h * half + lane + width], place_at(lon, h), c
                )
    relays = {}

    def relayed(c):
        for s in range(1, n_lon):
            source = lon_at(-s)
            relays[c, s].wait_recv()
            if aligned:
                lay_out(held(source, 1 - odd), place_at(source, 1 - odd), c)

    for c, (first, last) in enumerate(spans):
        for s in range(1, n_lon):
            source = lon_at(-s)
            gathers[c, s].wait_recv()
            part = dfull.at[source, odd, :, pl.ds(first, last - first)]
            copy = remote(part, part, relay_s.at[c, s - 1], relay_r.at[c, s - 1], at(lat, lon, pair))
            copy.start()
            relays[c, s] = copy
            if aligned:
                lay_out(held(source, odd), place_at(source, odd), c)
        if c > 0:
            relayed(c - 1)
    relayed(len(lanes) - 1)
    if not aligned:
        for copy in [*gathers.values(), *relays.values()]:
            copy.wait_send()
        for h in (0, 1):
            dfull[lon, h] = d_ref[:, h * half : (h + 1) * half]
            for c in range(len(lanes)):
                for owner in range(n_lon):
                    lay_out_small(owner, h, c)
        bhat[...] = stage[...].astype(BF16)

    def stack_codes(turn):
        for i, (h, a, b) in enumerate(COMBOS):
            for p in range(rows):
                zs[p * cols : (p + 1) * cols, i * atoms : (i + 1) * atoms] = zext[
                    turn, h, 1 + p - a, left - b : full - b, :
                ]
        return zs[...].astype(BF16)

    def residual(stacked):
        synth = jnp.dot(stacked, bhat[...], preferred_element_type=F32)
        return (synth - x_ref[...].astype(F32)).astype(BF16)

    shrink = STEP_SIZE * th_ref[...]
    momentum = 1.0
    for turn in range(ITERS):
        wait_all(halo, turn)
        resid = residual(stack_codes(turn))
        terms = contract(resid, bhat[...], 1, 1)
        cbuf[turn] = jnp.zeros_like(cbuf[turn])
        for i, (h, a, b) in enumerate(COMBOS):
            for p in range(rows):
                cbuf[turn, h, 1 + p - a, left - b : full - b, :] += terms[
                    p * cols : (p + 1) * cols, i * atoms : (i + 1) * atoms
                ]
        start_all(adjoint, turn)
        wait_all(adjoint, turn)
        later = (1.0 + math.sqrt(1.0 + 4.0 * momentum * momentum)) / 2.0
        weight = (momentum - 1.0) / later
        momentum = later
        for p in range(rows):
            total = cbuf[turn, 0, 1 + p, left:full, :] + qbuf[turn, 1, 1 + p, left:full, :]
            edge = qbuf[turn, 0, 1 + p, 0:8, :] + qbuf[turn, 1, 1 + p, 0:8, :]
            if p == rows - 1:
                total = total + qbuf[turn, 0, 0, left:full, :] + qbuf[turn, 1, 0, left:full, :]
                edge = edge + qbuf[turn, 0, 0, 0:8, :] + qbuf[turn, 1, 0, 0:8, :]
            acc[...] = total
            acc[cols - 8 : cols, :] += edge
            descent = moving[p] - STEP_SIZE * acc[...]
            updated = jnp.where(
                descent > shrink, descent - shrink, jnp.where(descent < -shrink, descent + shrink, 0.0)
            )
            ahead = updated + weight * (updated - current[p])
            moving[p] = ahead
            current[p] = updated
            set_codes(turn + 1, p, ahead if turn < ITERS - 1 else updated)
        start_all(halo, turn + 1)
    for p in range(rows):
        codes_ref[p * cols : (p + 1) * cols, :] = current[p]
    wait_all(halo, ITERS)
    stacked = stack_codes(ITERS)
    resid = residual(stacked)

    wide = 4 * atoms
    chunks = groups // 2
    for h in (0, 1):
        zh[h] = stacked[:, h * wide : (h + 1) * wide]
    part_of = [resid[:, j * 256 : (j + 1) * 256] for j in range(chunks)]
    pairs = []
    for j in range(chunks):
        away[j] = contract(zh[1 - odd], part_of[j], 0, 0)
        copy = remote(away.at[j], ra.at[j], a_s.at[j], a_r.at[j], at(lat, lon, pair))
        copy.start()
        pairs.append(copy)
    for j in range(chunks):
        home[j] = contract(zh[odd], part_of[j], 0, 0)
    eighth = upper * 4 + lat

    def lon_stage(j):
        pairs[j].wait()
        part = (home[j] + ra[j]).astype(BF16)
        cells = jnp.concatenate(
            [
                jnp.concatenate(
                    [part[ab * atoms : (ab + 1) * atoms, g * 128 : (g + 1) * 128] for ab in range(4)], axis=1
                )
                for g in (0, 1)
            ],
            axis=0,
        )
        plain = contract(cells, order, 1, 1)
        for tile in range(8):
            row, lane = tile // 4 * atoms, tile % 4 * 128
            for owner in range(n_lon):
                sb[j, tile, owner] = plain[
                    row + owner * owned : row + (owner + 1) * owned, lane : lane + 128
                ].astype(BF16)
        return [
            remote(
                sb.at[j, :, lon_at(s)], rb.at[s - 1, j], b_s.at[j, s - 1], b_r.at[j, s - 1], at(lat, lon_at(s), tm)
            )
            for s in range(1, n_lon)
        ]

    def cross_stage(j):
        total = sb[j, :, lon].astype(F32)
        for s in range(1, n_lon):
            total = total + rb[s - 1, j].astype(F32)
        sc[j] = total.astype(BF16)
        return [
            remote(sc.at[j, pl.ds((1 - upper) * 4, 4)], rc.at[j], c_s.at[j], c_r.at[j], at(lat, lon, cross))
        ]

    def lat_stage(j):
        sd[j] = (sc[j, pl.ds(upper * 4, 4)].astype(F32) + rc[j].astype(F32)).astype(BF16)
        copies = []
        for s in range(1, n_lat):
            to = lax.rem(lat + s, n_lat)
            copies.append(
                remote(sd.at[j, to], rd.at[s - 1, j], d_s.at[j, s - 1], d_r.at[j, s - 1], at(to, lon, tm))
            )
        return copies

    def lat_back(j):
        total = sd[j, lat].astype(F32)
        for s in range(1, n_lat):
            total = total + rd[s - 1, j].astype(F32)
        fin[odd, j, eighth] = total.astype(BF16)
        own = fin.at[odd, j, eighth]
        return [
            remote(own, own, e_s.at[j, s - 1], e_r.at[j, s - 1], at(lax.rem(lat + s, n_lat), lon, tm))
            for s in range(1, n_lat)
        ]

    def cross_back(j):
        own = fin.at[odd, j, pl.ds(upper * 4, 4)]
        return [remote(own, own, f_s.at[j], f_r.at[j], at(lat, lon, cross))]

    def pair_back(j):
        own = fin.at[odd, j]
        return [remote(own, own, g_s.at[j], g_r.at[j], at(lat, lon, pair))]

    def finish(j):
        for h in (0, 1):
            for tile in range(8):
                lane = (8 * j + tile) * 128
                if lane < half:
                    grad_ref[:, h * half + lane : h * half + lane + 128] = fin[h, j, tile]
        return []

    stages = [lon_stage, cross_stage, lat_stage, lat_back, cross_back, pair_back, finish]
    flying = {}
    for stage in stages:
        for j in range(chunks):
            for copy in flying.get(j, []):
                copy.wait()
            flying[j] = stage(j)
            for copy in flying[j]:
                copy.start()
    if aligned:
        for copy in [*gathers.values(), *relays.values()]:
            copy.wait_send()


def body(sizes, signal, dictionary, codes_init, thresholds):
    n_lat, n_lon, n_tm, atoms, rows, cols, half, padded = sizes
    channels = signal.shape[1]
    patch = channels * 16
    positions = rows * cols
    owned = dictionary.shape[0]
    target = signal[0].reshape(channels, rows, 4, cols, 4).transpose(1, 3, 0, 2, 4).reshape(positions, patch)
    target = jnp.pad(target, ((0, 0), (0, padded - patch)))
    start = codes_init[0].reshape(atoms, positions).T
    order = jnp.asarray(cell_order(), BF16)
    ext = (2, rows + 1, 8 + cols, atoms)
    dma = pltpu.SemaphoreType.DMA
    chunks, spans = padded // 256, -(-padded // 512)
    codes, grad = pl.pallas_call(
        functools.partial(kernel, sizes),
        out_shape=(
            jax.ShapeDtypeStruct((positions, atoms), F32),
            jax.ShapeDtypeStruct(dictionary.shape, BF16),
        ),
        in_specs=[pl.BlockSpec(memory_space=pltpu.VMEM)] * 5,
        out_specs=(pl.BlockSpec(memory_space=pltpu.VMEM),) * 2,
        scratch_shapes=[
            pltpu.VMEM((n_lon, 2, owned, half), BF16),
            pltpu.VMEM((8 * atoms, padded), BF16),
            pltpu.VMEM((8, 128) if owned % 16 == 0 else (8 * atoms, padded), F32),
            pltpu.VMEM((ITERS + 1,) + ext, F32),
            pltpu.VMEM((positions, 8 * atoms), F32),
            pltpu.VMEM((ITERS,) + ext, F32),
            pltpu.VMEM((ITERS,) + ext, F32),
            pltpu.VMEM((cols, atoms), F32),
            pltpu.VMEM((rows, cols, atoms), F32),
            pltpu.VMEM((rows, cols, atoms), F32),
            pltpu.VMEM((2, positions, 4 * atoms), BF16),
            pltpu.VMEM((chunks, 4 * atoms, 256), F32),
            pltpu.VMEM((chunks, 4 * atoms, 256), F32),
            pltpu.VMEM((chunks, 4 * atoms, 256), F32),
            pltpu.VMEM((chunks, 8, n_lon, owned, 128), BF16),
            pltpu.VMEM((n_lon - 1, chunks, 8, owned, 128), BF16),
            pltpu.VMEM((chunks, 8, owned, 128), BF16),
            pltpu.VMEM((chunks, 4, owned, 128), BF16),
            pltpu.VMEM((chunks, 4, owned, 128), BF16),
            pltpu.VMEM((n_lat - 1, chunks, owned, 128), BF16),
            pltpu.VMEM((2, chunks, 8, owned, 128), BF16),
            dma((spans, n_lon - 1)), dma((spans, n_lon - 1)), dma((spans, n_lon - 1)), dma((spans, n_lon - 1)),
            dma((ITERS + 1, 8)), dma((ITERS + 1, 8)), dma((ITERS, 8)), dma((ITERS, 8)),
            dma((chunks,)), dma((chunks,)), dma((chunks, n_lon - 1)), dma((chunks, n_lon - 1)),
            dma((chunks,)), dma((chunks,)),
            dma((chunks, n_lat - 1)), dma((chunks, n_lat - 1)), dma((chunks, n_lat - 1)), dma((chunks, n_lat - 1)),
            dma((chunks,)), dma((chunks,)), dma((chunks,)), dma((chunks,)),
        ],
        compiler_params=pltpu.CompilerParams(
            collective_id=0, has_side_effects=True, vmem_limit_bytes=48 * 2**20
        ),
        cost_estimate=pl.CostEstimate(flops=10**9, bytes_accessed=4 * 10**6, transcendentals=0),
    )(dictionary, order, target, start, thresholds[None, :])
    scale = 1.0 / math.sqrt(n_tm * n_lat * n_lon * positions)
    return codes.T.reshape(1, atoms, rows, cols), grad.astype(F32) * scale


def solution(mesh):
    n_lat, n_lon, n_tm = mesh.shape["lat"], mesh.shape["lon"], mesh.shape["tm"]
    assert n_lat == 4 and n_tm == 4 and n_lon >= 2
    placed = (P("tm", None, "lat", "lon"), P("lon", None), P("tm", None, "lat", "lon"), P())

    def part(signal, dictionary, codes_init, thresholds):
        atoms, rows, cols = codes_init.shape[1:]
        half = dictionary.shape[1] // 2
        sizes = (n_lat, n_lon, n_tm, atoms, rows, cols, half, -(-half // GROUP) * 128)
        return body(sizes, signal, dictionary, codes_init, thresholds)

    return jax.shard_map(
        part,
        mesh=mesh,
        in_specs=placed,
        out_specs=(P("tm", None, "lat", "lon"), P("lon", None)),
        check_vma=False,
    )
```

```python
import functools
import math

import jax
import jax.numpy as jnp
import numpy as np
from jax import lax
from jax.experimental import pallas as pl
from jax.experimental.pallas import tpu as pltpu
from jax.sharding import PartitionSpec as P

ITERS = 2
STEP_SIZE = 0.5
MESH = pl.DeviceIdType.MESH
F32, BF16 = jnp.float32, jnp.bfloat16
COMBOS = [(h, a, b) for h in (0, 1) for a in (0, 1) for b in (0, 1)]
AROUND = sorted(
    [(t, a, b) for t in (-1, 0, 1) for a in (-1, 0, 1) for b in (-1, 0, 1) if (t, a, b) != (0, 0, 0)],
    key=lambda e: abs(e[0]) + abs(e[1]) + abs(e[2]),
)
GROUP = 512


def cell_order():
    c, a, u, b, v = np.meshgrid(*[np.arange(n) for n in (8, 2, 4, 2, 4)], indexing="ij")
    source = ((((c * 2 + a) * 4 + u) * 2 + b) * 4 + v).ravel()
    target = ((((a * 2 + b) * 8 + c) * 4 + u) * 4 + v).ravel()
    order = np.zeros((GROUP, GROUP), np.float32)
    order[source, target] = 1.0
    return order


def contract(x, y, dx, dy):
    return lax.dot_general(x, y, (((dx,), (dy,)), ((), ())), preferred_element_type=F32)


def kernel(
    sizes, d_ref, p_ref, x_ref, z0_ref, th_ref, codes_ref, grad_ref,
    dfull, bhat, stage, zs, cbuf, qbuf, acc, moving, current,
    zh, away, home, ra, sb, rb, sc, rc, sd, rd, fin,
    dict_s, dict_r, relay_s, relay_r, halo_s, halo_r, adj_s, adj_r,
    a_s, a_r, b_s, b_r, c_s, c_r, d_s, d_r, e_s, e_r, f_s, f_r, g_s, g_r,
):
    n_lat, n_lon, n_tm, atoms, rows, cols, half, padded = sizes
    owned = atoms // n_lon
    lat, lon, tm = lax.axis_index("lat"), lax.axis_index("lon"), lax.axis_index("tm")
    left = 8
    full = left + cols
    groups = padded // 128

    def at(la, lo, t):
        return (la, lo, t)

    def remote(src, dst, send, recv, where):
        return pltpu.make_async_remote_copy(
            src_ref=src, dst_ref=dst, send_sem=send, recv_sem=recv, device_id=where, device_id_type=MESH
        )

    def lon_at(step):
        return lax.rem(lon + step + n_lon, n_lon)

    current[...] = jnp.zeros_like(current)
    for p in range(rows):
        current[0, 1 + p, left:full, :] = z0_ref[p * cols : (p + 1) * cols, :]

    barrier = pltpu.get_barrier_semaphore()
    count = n_lat * n_lon * n_tm
    mine = (lat * n_lon + lon) * n_tm + tm

    def greet(step, carry):
        other = lax.rem(mine + step, count)
        where = (other // (n_lon * n_tm), lax.rem(other // n_tm, n_lon), lax.rem(other, n_tm))
        pl.semaphore_signal(barrier, inc=1, device_id=where, device_id_type=MESH)
        return carry

    lax.fori_loop(1, count, greet, 0)
    pl.semaphore_wait(barrier, count - 1)

    odd = lax.rem(tm, 2)
    upper = tm // 2
    pair = tm + 1 - 2 * odd
    cross = tm + 2 - 4 * upper

    def region(ref, head, da, dl, sender):
        r = (pl.ds(rows if sender else 0, 1)) if da else pl.ds(1, rows)
        c = (pl.ds(full - 8 if sender else 0, 8)) if dl else pl.ds(left, cols)
        return ref.at[head + (r, c)]

    def halo(m):
        dt, da, dl = COMBOS[m]
        copy = remote(
            region(current, (0,), da, dl, True), region(current, (dt,), da, dl, False), halo_s.at[m], halo_r.at[m],
            at(lax.rem(lat + da, n_lat), lon_at(dl), lax.rem(tm + dt, n_tm)),
        )
        sends = (tm + dt < n_tm) & (lat + da < n_lat)
        gets = (tm - dt >= 0) & (lat - da >= 0)
        return copy, sends, gets

    def facing(et, ea, el, sender):
        h = pl.ds(0, 2) if et == 0 else pl.ds(1 if (et > 0) == sender else 0, 1)
        r = pl.ds(0, rows + 1) if ea == 0 else pl.ds(0 if (ea > 0) == sender else rows, 1)
        c = pl.ds(0, full) if el == 0 else pl.ds(0 if (el > 0) == sender else full - 8, 8)
        return h, r, c

    def inside(et, ea):
        return (tm + et >= 0) & (tm + et < n_tm) & (lat + ea >= 0) & (lat + ea < n_lat)

    def adjoint(turn, m):
        et, ea, el = AROUND[m]
        copy = remote(
            cbuf.at[(turn,) + facing(et, ea, el, True)], qbuf.at[(turn, m) + facing(et, ea, el, False)],
            adj_s.at[turn, m], adj_r.at[turn, m],
            at(lax.rem(lat - ea + n_lat, n_lat), lon_at(-el), lax.rem(tm - et + n_tm, n_tm)),
        )
        return copy, inside(-et, -ea), inside(et, ea)

    lanes = [(g, min(g + 4, groups)) for g in range(0, groups, 4)]
    spans = [(g0 * GROUP, min(g1 * GROUP, half)) for g0, g1 in lanes]
    gathers = {}
    for c, (first, last) in enumerate(spans):
        for s in range(1, n_lon):
            copy = remote(
                d_ref.at[:, pl.ds(pl.multiple_of(odd * half + first, 128), last - first)],
                dfull.at[lon, odd, :, pl.ds(first, last - first)],
                dict_s.at[c, s - 1], dict_r.at[c, s - 1], at(lat, lon_at(s), tm),
            )
            copy.start()
            gathers[c, s] = copy
        if c == 0:
            for m in range(1, 8):
                copy, sends, _ = halo(m)
                pl.when(sends)(copy.start)

    order = p_ref[...]

    def lay_out(load, place, chunk):
        g0, g1 = lanes[chunk]
        pieces = []
        for g in range(g0, g1):
            width = min(GROUP, half - g * GROUP)
            piece = load(g * GROUP, width)
            if width < GROUP:
                piece = jnp.concatenate([piece, jnp.zeros((owned, GROUP - width), BF16)], axis=1)
            pieces.append(piece)
        cells = jnp.dot(jnp.concatenate(pieces, axis=0), order, preferred_element_type=F32)
        for g in range(g0, g1):
            for ab in range(4):
                place(ab * atoms, g * 128, cells[(g - g0) * owned : (g - g0 + 1) * owned, ab * 128 : (ab + 1) * 128])

    aligned = owned % 16 == 0

    def place_at(owner, h):
        def place(row, lane, value):
            if aligned:
                start = pl.multiple_of(h * 4 * atoms + row + owner * owned, 16)
                bhat[pl.ds(start, owned), lane : lane + 128] = value.astype(BF16)
            else:
                start = h * 4 * atoms + row + owner * owned
                stage[start : start + owned, lane : lane + 128] = value
        return place

    def lay_out_small(owner, h, chunk):
        for g in range(*lanes[chunk]):
            width = min(GROUP, half - g * GROUP)
            cells = jnp.dot(held(owner, h)(g * GROUP, width), order[:width], preferred_element_type=F32)
            for ab in range(4):
                place_at(owner, h)(ab * atoms, g * 128, cells[:, ab * 128 : (ab + 1) * 128])

    def held(owner, h):
        return lambda lane, width: dfull[owner, h, :, lane : lane + width]

    if aligned:
        for c in range(len(lanes)):
            for h in (0, 1):
                lay_out(
                    lambda lane, width: d_ref[:, h * half + lane : h * half + lane + width], place_at(lon, h), c
                )
    relays = {}

    def relayed(c):
        for s in range(1, n_lon):
            source = lon_at(-s)
            relays[c, s].wait_recv()
            if aligned:
                lay_out(held(source, 1 - odd), place_at(source, 1 - odd), c)

    for c, (first, last) in enumerate(spans):
        for s in range(1, n_lon):
            source = lon_at(-s)
            gathers[c, s].wait_recv()
            part = dfull.at[source, odd, :, pl.ds(first, last - first)]
            copy = remote(part, part, relay_s.at[c, s - 1], relay_r.at[c, s - 1], at(lat, lon, pair))
            copy.start()
            relays[c, s] = copy
            if aligned:
                lay_out(held(source, odd), place_at(source, odd), c)
        if c > 0:
            relayed(c - 1)
    relayed(len(lanes) - 1)
    if not aligned:
        for copy in [*gathers.values(), *relays.values()]:
            copy.wait_send()
        for h in (0, 1):
            dfull[lon, h] = d_ref[:, h * half : (h + 1) * half]
            for c in range(len(lanes)):
                for owner in range(n_lon):
                    lay_out_small(owner, h, c)
        bhat[...] = stage[...].astype(BF16)

    def stack_codes(held):
        for i, (h, a, b) in enumerate(COMBOS):
            for p in range(rows):
                zs[p * cols : (p + 1) * cols, i * atoms : (i + 1) * atoms] = held[
                    h, 1 + p - a, left - b : full - b, :
                ]
        return zs[...].astype(BF16)

    def residual(stacked):
        synth = jnp.dot(stacked, bhat[...], preferred_element_type=F32)
        return (synth - x_ref[...].astype(F32)).astype(BF16)

    shrink = STEP_SIZE * th_ref[...]
    momentum = 1.0
    first_hour = jnp.where(tm > 0, 1.0, 0.0)
    first_band = jnp.where(lat > 0, 1.0, 0.0)
    for m in range(1, 8):
        copy, sends, gets = halo(m)
        pl.when(gets)(copy.wait_recv)
        pl.when(sends)(copy.wait_send)
    moving[...] = current[...]
    for turn in range(ITERS):
        resid = residual(stack_codes(moving))
        terms = contract(resid, bhat[...], 1, 1)
        cbuf[turn] = jnp.zeros_like(cbuf[turn])
        for i, (h, a, b) in enumerate(COMBOS):
            for p in range(rows):
                cbuf[turn, h, 1 + p - a, left - b : full - b, :] += terms[
                    p * cols : (p + 1) * cols, i * atoms : (i + 1) * atoms
                ]
        for m in reversed(range(len(AROUND))):
            copy, sends, _ = adjoint(turn, m)
            pl.when(sends)(copy.start)
        acc[...] = cbuf[turn]
        for m in range(len(AROUND)):
            copy, _, gets = adjoint(turn, m)

            def add(copy=copy, m=m):
                copy.wait_recv()
                h, r, c = facing(*AROUND[m], False)
                acc[h, r, c, :] += qbuf[turn, m, h, r, c, :]

            pl.when(gets)(add)
        later = (1.0 + math.sqrt(1.0 + 4.0 * momentum * momentum)) / 2.0
        weight = (momentum - 1.0) / later
        momentum = later
        for h in (0, 1):
            for r in range(rows + 1):
                descent = moving[h, r] - STEP_SIZE * acc[h, r]
                updated = jnp.where(
                    descent > shrink, descent - shrink, jnp.where(descent < -shrink, descent + shrink, 0.0)
                )
                if h:
                    updated = updated * first_hour
                if r == 0:
                    updated = updated * first_band
                moving[h, r] = updated + weight * (updated - current[h, r])
                current[h, r] = updated
    for p in range(rows):
        codes_ref[p * cols : (p + 1) * cols, :] = current[0, 1 + p, left:full, :]
    stacked = stack_codes(current)
    resid = residual(stacked)

    wide = 4 * atoms
    chunks = groups // 2
    for h in (0, 1):
        zh[h] = stacked[:, h * wide : (h + 1) * wide]
    part_of = [resid[:, j * 256 : (j + 1) * 256] for j in range(chunks)]
    pairs = []
    for j in range(chunks):
        away[j] = contract(zh[1 - odd], part_of[j], 0, 0)
        copy = remote(away.at[j], ra.at[j], a_s.at[j], a_r.at[j], at(lat, lon, pair))
        copy.start()
        pairs.append(copy)
    for j in range(chunks):
        home[j] = contract(zh[odd], part_of[j], 0, 0)
    eighth = upper * 4 + lat

    def lon_stage(j):
        pairs[j].wait()
        part = (home[j] + ra[j]).astype(BF16)
        cells = jnp.concatenate(
            [
                jnp.concatenate(
                    [part[ab * atoms : (ab + 1) * atoms, g * 128 : (g + 1) * 128] for ab in range(4)], axis=1
                )
                for g in (0, 1)
            ],
            axis=0,
        )
        plain = contract(cells, order, 1, 1)
        for tile in range(8):
            row, lane = tile // 4 * atoms, tile % 4 * 128
            for owner in range(n_lon):
                sb[j, tile, owner] = plain[
                    row + owner * owned : row + (owner + 1) * owned, lane : lane + 128
                ].astype(BF16)
        return [
            remote(
                sb.at[j, :, lon_at(s)], rb.at[s - 1, j], b_s.at[j, s - 1], b_r.at[j, s - 1], at(lat, lon_at(s), tm)
            )
            for s in range(1, n_lon)
        ]

    def cross_stage(j):
        total = sb[j, :, lon].astype(F32)
        for s in range(1, n_lon):
            total = total + rb[s - 1, j].astype(F32)
        sc[j] = total.astype(BF16)
        return [
            remote(sc.at[j, pl.ds((1 - upper) * 4, 4)], rc.at[j], c_s.at[j], c_r.at[j], at(lat, lon, cross))
        ]

    def lat_stage(j):
        sd[j] = (sc[j, pl.ds(upper * 4, 4)].astype(F32) + rc[j].astype(F32)).astype(BF16)
        copies = []
        for s in range(1, n_lat):
            to = lax.rem(lat + s, n_lat)
            copies.append(
                remote(sd.at[j, to], rd.at[s - 1, j], d_s.at[j, s - 1], d_r.at[j, s - 1], at(to, lon, tm))
            )
        return copies

    def lat_back(j):
        total = sd[j, lat].astype(F32)
        for s in range(1, n_lat):
            total = total + rd[s - 1, j].astype(F32)
        fin[odd, j, eighth] = total.astype(BF16)
        own = fin.at[odd, j, eighth]
        return [
            remote(own, own, e_s.at[j, s - 1], e_r.at[j, s - 1], at(lax.rem(lat + s, n_lat), lon, tm))
            for s in range(1, n_lat)
        ]

    def cross_back(j):
        own = fin.at[odd, j, pl.ds(upper * 4, 4)]
        return [remote(own, own, f_s.at[j], f_r.at[j], at(lat, lon, cross))]

    def pair_back(j):
        own = fin.at[odd, j]
        return [remote(own, own, g_s.at[j], g_r.at[j], at(lat, lon, pair))]

    def finish(j):
        for h in (0, 1):
            for tile in range(8):
                lane = (8 * j + tile) * 128
                if lane < half:
                    grad_ref[:, h * half + lane : h * half + lane + 128] = fin[h, j, tile]
        return []

    stages = [lon_stage, cross_stage, lat_stage, lat_back, cross_back, pair_back, finish]
    flying = {}
    for stage in stages:
        for j in range(chunks):
            for copy in flying.get(j, []):
                copy.wait()
            flying[j] = stage(j)
            for copy in flying[j]:
                copy.start()
    for turn in range(ITERS):
        for m in range(len(AROUND)):
            copy, sends, _ = adjoint(turn, m)
            pl.when(sends)(copy.wait_send)
    if aligned:
        for copy in [*gathers.values(), *relays.values()]:
            copy.wait_send()


def body(sizes, signal, dictionary, codes_init, thresholds):
    n_lat, n_lon, n_tm, atoms, rows, cols, half, padded = sizes
    channels = signal.shape[1]
    patch = channels * 16
    positions = rows * cols
    owned = dictionary.shape[0]
    target = signal[0].reshape(channels, rows, 4, cols, 4).transpose(1, 3, 0, 2, 4).reshape(positions, patch)
    target = jnp.pad(target, ((0, 0), (0, padded - patch)))
    start = codes_init[0].reshape(atoms, positions).T
    order = jnp.asarray(cell_order(), BF16)
    ext = (2, rows + 1, 8 + cols, atoms)
    dma = pltpu.SemaphoreType.DMA
    chunks, spans = padded // 256, -(-padded // 512)
    codes, grad = pl.pallas_call(
        functools.partial(kernel, sizes),
        out_shape=(
            jax.ShapeDtypeStruct((positions, atoms), F32),
            jax.ShapeDtypeStruct(dictionary.shape, BF16),
        ),
        in_specs=[pl.BlockSpec(memory_space=pltpu.VMEM)] * 5,
        out_specs=(pl.BlockSpec(memory_space=pltpu.VMEM),) * 2,
        scratch_shapes=[
            pltpu.VMEM((n_lon, 2, owned, half), BF16),
            pltpu.VMEM((8 * atoms, padded), BF16),
            pltpu.VMEM((8, 128) if owned % 16 == 0 else (8 * atoms, padded), F32),
            pltpu.VMEM((positions, 8 * atoms), F32),
            pltpu.VMEM((ITERS,) + ext, F32),
            pltpu.VMEM((ITERS, len(AROUND)) + ext, F32),
            pltpu.VMEM(ext, F32),
            pltpu.VMEM(ext, F32),
            pltpu.VMEM(ext, F32),
            pltpu.VMEM((2, positions, 4 * atoms), BF16),
            pltpu.VMEM((chunks, 4 * atoms, 256), F32),
            pltpu.VMEM((chunks, 4 * atoms, 256), F32),
            pltpu.VMEM((chunks, 4 * atoms, 256), F32),
            pltpu.VMEM((chunks, 8, n_lon, owned, 128), BF16),
            pltpu.VMEM((n_lon - 1, chunks, 8, owned, 128), BF16),
            pltpu.VMEM((chunks, 8, owned, 128), BF16),
            pltpu.VMEM((chunks, 4, owned, 128), BF16),
            pltpu.VMEM((chunks, 4, owned, 128), BF16),
            pltpu.VMEM((n_lat - 1, chunks, owned, 128), BF16),
            pltpu.VMEM((2, chunks, 8, owned, 128), BF16),
            dma((spans, n_lon - 1)), dma((spans, n_lon - 1)), dma((spans, n_lon - 1)), dma((spans, n_lon - 1)),
            dma((8,)), dma((8,)), dma((ITERS, len(AROUND))), dma((ITERS, len(AROUND))),
            dma((chunks,)), dma((chunks,)), dma((chunks, n_lon - 1)), dma((chunks, n_lon - 1)),
            dma((chunks,)), dma((chunks,)),
            dma((chunks, n_lat - 1)), dma((chunks, n_lat - 1)), dma((chunks, n_lat - 1)), dma((chunks, n_lat - 1)),
            dma((chunks,)), dma((chunks,)), dma((chunks,)), dma((chunks,)),
        ],
        compiler_params=pltpu.CompilerParams(
            collective_id=0, has_side_effects=True, vmem_limit_bytes=48 * 2**20
        ),
        cost_estimate=pl.CostEstimate(flops=10**9, bytes_accessed=4 * 10**6, transcendentals=0),
    )(dictionary, order, target, start, thresholds[None, :])
    scale = 1.0 / math.sqrt(n_tm * n_lat * n_lon * positions)
    return codes.T.reshape(1, atoms, rows, cols), grad.astype(F32) * scale


def solution(mesh):
    n_lat, n_lon, n_tm = mesh.shape["lat"], mesh.shape["lon"], mesh.shape["tm"]
    assert n_lat == 4 and n_tm == 4 and n_lon >= 2
    placed = (P("tm", None, "lat", "lon"), P("lon", None), P("tm", None, "lat", "lon"), P())

    def part(signal, dictionary, codes_init, thresholds):
        atoms, rows, cols = codes_init.shape[1:]
        half = dictionary.shape[1] // 2
        sizes = (n_lat, n_lon, n_tm, atoms, rows, cols, half, -(-half // GROUP) * 128)
        return body(sizes, signal, dictionary, codes_init, thresholds)

    return jax.shard_map(
        part,
        mesh=mesh,
        in_specs=placed,
        out_specs=(P("tm", None, "lat", "lon"), P("lon", None)),
        check_vma=False,
    )
```

```python
import functools
import math

import jax
import jax.numpy as jnp
import numpy as np
from jax import lax
from jax.experimental import pallas as pl
from jax.experimental.pallas import tpu as pltpu
from jax.sharding import PartitionSpec as P

ITERS = 2
STEP_SIZE = 0.5
MESH = pl.DeviceIdType.MESH
F32, BF16 = jnp.float32, jnp.bfloat16
COMBOS = [(h, a, b) for h in (0, 1) for a in (0, 1) for b in (0, 1)]
AROUND = sorted(
    [(t, a, b) for t in (-1, 0, 1) for a in (-1, 0, 1) for b in (-1, 0, 1) if (t, a, b) != (0, 0, 0)],
    key=lambda e: abs(e[0]) + abs(e[1]) + abs(e[2]),
)
GROUP = 512


def cell_order():
    c, a, u, b, v = np.meshgrid(*[np.arange(n) for n in (8, 2, 4, 2, 4)], indexing="ij")
    source = ((((c * 2 + a) * 4 + u) * 2 + b) * 4 + v).ravel()
    target = ((((a * 2 + b) * 8 + c) * 4 + u) * 4 + v).ravel()
    order = np.zeros((GROUP, GROUP), np.float32)
    order[source, target] = 1.0
    return order


def contract(x, y, dx, dy):
    return lax.dot_general(x, y, (((dx,), (dy,)), ((), ())), preferred_element_type=F32)


def kernel(
    sizes, d_ref, p_ref, x_ref, z0_ref, th_ref, codes_ref, grad_ref,
    dfull, bhat, stage, zs, cbuf, qbuf, acc, moving, current,
    zh, away, home, ra, sb, rb, sc, home8, rd, fin,
    dict_s, dict_r, relay_s, relay_r, halo_s, halo_r, adj_s, adj_r,
    a_s, a_r, b_s, b_r, d_s, d_r, e_s, e_r, g_s, g_r,
):
    n_lat, n_lon, n_tm, atoms, rows, cols, half, padded = sizes
    owned = atoms // n_lon
    lat, lon, tm = lax.axis_index("lat"), lax.axis_index("lon"), lax.axis_index("tm")
    left = 8
    full = left + cols
    groups = padded // 128

    def at(la, lo, t):
        return (la, lo, t)

    def remote(src, dst, send, recv, where):
        return pltpu.make_async_remote_copy(
            src_ref=src, dst_ref=dst, send_sem=send, recv_sem=recv, device_id=where, device_id_type=MESH
        )

    def lon_at(step):
        return lax.rem(lon + step + n_lon, n_lon)

    current[...] = jnp.zeros_like(current)
    for p in range(rows):
        current[0, 1 + p, left:full, :] = z0_ref[p * cols : (p + 1) * cols, :]

    barrier = pltpu.get_barrier_semaphore()
    count = n_lat * n_lon * n_tm
    mine = (lat * n_lon + lon) * n_tm + tm

    def greet(step, carry):
        other = lax.rem(mine + step, count)
        where = (other // (n_lon * n_tm), lax.rem(other // n_tm, n_lon), lax.rem(other, n_tm))
        pl.semaphore_signal(barrier, inc=1, device_id=where, device_id_type=MESH)
        return carry

    lax.fori_loop(1, count, greet, 0)
    pl.semaphore_wait(barrier, count - 1)

    odd = lax.rem(tm, 2)
    upper = tm // 2
    pair = tm + 1 - 2 * odd
    cross = tm + 2 - 4 * upper

    def region(ref, head, da, dl, sender):
        r = (pl.ds(rows if sender else 0, 1)) if da else pl.ds(1, rows)
        c = (pl.ds(full - 8 if sender else 0, 8)) if dl else pl.ds(left, cols)
        return ref.at[head + (r, c)]

    def halo(m):
        dt, da, dl = COMBOS[m]
        copy = remote(
            region(current, (0,), da, dl, True), region(current, (dt,), da, dl, False), halo_s.at[m], halo_r.at[m],
            at(lax.rem(lat + da, n_lat), lon_at(dl), lax.rem(tm + dt, n_tm)),
        )
        sends = (tm + dt < n_tm) & (lat + da < n_lat)
        gets = (tm - dt >= 0) & (lat - da >= 0)
        return copy, sends, gets

    def facing(et, ea, el, sender):
        h = pl.ds(0, 2) if et == 0 else pl.ds(1 if (et > 0) == sender else 0, 1)
        r = pl.ds(0, rows + 1) if ea == 0 else pl.ds(0 if (ea > 0) == sender else rows, 1)
        c = pl.ds(0, full) if el == 0 else pl.ds(0 if (el > 0) == sender else full - 8, 8)
        return h, r, c

    def inside(et, ea):
        return (tm + et >= 0) & (tm + et < n_tm) & (lat + ea >= 0) & (lat + ea < n_lat)

    def adjoint(turn, m):
        et, ea, el = AROUND[m]
        copy = remote(
            cbuf.at[(turn,) + facing(et, ea, el, True)], qbuf.at[(turn, m) + facing(et, ea, el, False)],
            adj_s.at[turn, m], adj_r.at[turn, m],
            at(lax.rem(lat - ea + n_lat, n_lat), lon_at(-el), lax.rem(tm - et + n_tm, n_tm)),
        )
        return copy, inside(-et, -ea), inside(et, ea)

    lanes = [(g, min(g + 4, groups)) for g in range(0, groups, 4)]
    spans = [(g0 * GROUP, min(g1 * GROUP, half)) for g0, g1 in lanes]
    gathers = {}
    for c, (first, last) in enumerate(spans):
        for s in range(1, n_lon):
            copy = remote(
                d_ref.at[:, pl.ds(pl.multiple_of(odd * half + first, 128), last - first)],
                dfull.at[lon, odd, :, pl.ds(first, last - first)],
                dict_s.at[c, s - 1], dict_r.at[c, s - 1], at(lat, lon_at(s), tm),
            )
            copy.start()
            gathers[c, s] = copy
        if c == 0:
            for m in range(1, 8):
                copy, sends, _ = halo(m)
                pl.when(sends)(copy.start)

    order = p_ref[...]

    def lay_out(load, place, chunk):
        g0, g1 = lanes[chunk]
        pieces = []
        for g in range(g0, g1):
            width = min(GROUP, half - g * GROUP)
            piece = load(g * GROUP, width)
            if width < GROUP:
                piece = jnp.concatenate([piece, jnp.zeros((owned, GROUP - width), BF16)], axis=1)
            pieces.append(piece)
        cells = jnp.dot(jnp.concatenate(pieces, axis=0), order, preferred_element_type=F32)
        for g in range(g0, g1):
            for ab in range(4):
                place(ab * atoms, g * 128, cells[(g - g0) * owned : (g - g0 + 1) * owned, ab * 128 : (ab + 1) * 128])

    aligned = owned % 16 == 0

    def place_at(owner, h):
        def place(row, lane, value):
            if aligned:
                start = pl.multiple_of(h * 4 * atoms + row + owner * owned, 16)
                bhat[pl.ds(start, owned), lane : lane + 128] = value.astype(BF16)
            else:
                start = h * 4 * atoms + row + owner * owned
                stage[start : start + owned, lane : lane + 128] = value
        return place

    def lay_out_small(owner, h, chunk):
        for g in range(*lanes[chunk]):
            width = min(GROUP, half - g * GROUP)
            cells = jnp.dot(held(owner, h)(g * GROUP, width), order[:width], preferred_element_type=F32)
            for ab in range(4):
                place_at(owner, h)(ab * atoms, g * 128, cells[:, ab * 128 : (ab + 1) * 128])

    def held(owner, h):
        return lambda lane, width: dfull[owner, h, :, lane : lane + width]

    if aligned:
        for c in range(len(lanes)):
            for h in (0, 1):
                lay_out(
                    lambda lane, width: d_ref[:, h * half + lane : h * half + lane + width], place_at(lon, h), c
                )
    relays = {}

    def relayed(c):
        for s in range(1, n_lon):
            source = lon_at(-s)
            relays[c, s].wait_recv()
            if aligned:
                lay_out(held(source, 1 - odd), place_at(source, 1 - odd), c)

    for c, (first, last) in enumerate(spans):
        for s in range(1, n_lon):
            source = lon_at(-s)
            gathers[c, s].wait_recv()
            part = dfull.at[source, odd, :, pl.ds(first, last - first)]
            copy = remote(part, part, relay_s.at[c, s - 1], relay_r.at[c, s - 1], at(lat, lon, pair))
            copy.start()
            relays[c, s] = copy
            if aligned:
                lay_out(held(source, odd), place_at(source, odd), c)
        if c > 0:
            relayed(c - 1)
    relayed(len(lanes) - 1)
    if not aligned:
        for copy in [*gathers.values(), *relays.values()]:
            copy.wait_send()
        for h in (0, 1):
            dfull[lon, h] = d_ref[:, h * half : (h + 1) * half]
            for c in range(len(lanes)):
                for owner in range(n_lon):
                    lay_out_small(owner, h, c)
        bhat[...] = stage[...].astype(BF16)

    def stack_codes(held):
        for i, (h, a, b) in enumerate(COMBOS):
            for p in range(rows):
                zs[p * cols : (p + 1) * cols, i * atoms : (i + 1) * atoms] = held[
                    h, 1 + p - a, left - b : full - b, :
                ]
        return zs[...].astype(BF16)

    def residual(stacked):
        synth = jnp.dot(stacked, bhat[...], preferred_element_type=F32)
        return (synth - x_ref[...].astype(F32)).astype(BF16)

    shrink = STEP_SIZE * th_ref[...]
    momentum = 1.0
    first_hour = jnp.where(tm > 0, 1.0, 0.0)
    first_band = jnp.where(lat > 0, 1.0, 0.0)
    for m in range(1, 8):
        copy, sends, gets = halo(m)
        pl.when(gets)(copy.wait_recv)
        pl.when(sends)(copy.wait_send)
    moving[...] = current[...]
    for turn in range(ITERS):
        resid = residual(stack_codes(moving))
        terms = contract(resid, bhat[...], 1, 1)
        cbuf[turn] = jnp.zeros_like(cbuf[turn])
        for i, (h, a, b) in enumerate(COMBOS):
            for p in range(rows):
                cbuf[turn, h, 1 + p - a, left - b : full - b, :] += terms[
                    p * cols : (p + 1) * cols, i * atoms : (i + 1) * atoms
                ]
        for m in reversed(range(len(AROUND))):
            copy, sends, _ = adjoint(turn, m)
            pl.when(sends)(copy.start)
        acc[...] = cbuf[turn]
        for m in range(len(AROUND)):
            copy, _, gets = adjoint(turn, m)

            def add(copy=copy, m=m):
                copy.wait_recv()
                h, r, c = facing(*AROUND[m], False)
                acc[h, r, c, :] += qbuf[turn, m, h, r, c, :]

            pl.when(gets)(add)
        later = (1.0 + math.sqrt(1.0 + 4.0 * momentum * momentum)) / 2.0
        weight = (momentum - 1.0) / later
        momentum = later
        for h in (0, 1):
            for r in range(rows + 1):
                descent = moving[h, r] - STEP_SIZE * acc[h, r]
                updated = jnp.where(
                    descent > shrink, descent - shrink, jnp.where(descent < -shrink, descent + shrink, 0.0)
                )
                if h:
                    updated = updated * first_hour
                if r == 0:
                    updated = updated * first_band
                moving[h, r] = updated + weight * (updated - current[h, r])
                current[h, r] = updated
    for p in range(rows):
        codes_ref[p * cols : (p + 1) * cols, :] = current[0, 1 + p, left:full, :]
    stacked = stack_codes(current)
    resid = residual(stacked)

    wide = 4 * atoms
    chunks = groups // 2
    for h in (0, 1):
        zh[h] = stacked[:, h * wide : (h + 1) * wide]
    part_of = [resid[:, j * 256 : (j + 1) * 256] for j in range(chunks)]
    pairs = []
    for j in range(chunks):
        away[j] = contract(zh[1 - odd], part_of[j], 0, 0)
        copy = remote(away.at[j], ra.at[j], a_s.at[j], a_r.at[j], at(lat, lon, pair))
        copy.start()
        pairs.append(copy)
    for j in range(chunks):
        home[j] = contract(zh[odd], part_of[j], 0, 0)
    eighth = upper * 4 + lat

    def lon_stage(j):
        pairs[j].wait()
        part = (home[j] + ra[j]).astype(BF16)
        cells = jnp.concatenate(
            [
                jnp.concatenate(
                    [part[ab * atoms : (ab + 1) * atoms, g * 128 : (g + 1) * 128] for ab in range(4)], axis=1
                )
                for g in (0, 1)
            ],
            axis=0,
        )
        plain = contract(cells, order, 1, 1)
        for tile in range(8):
            row, lane = tile // 4 * atoms, tile % 4 * 128
            for owner in range(n_lon):
                sb[j, tile, owner] = plain[
                    row + owner * owned : row + (owner + 1) * owned, lane : lane + 128
                ].astype(BF16)
        return [
            remote(
                sb.at[j, :, lon_at(s)], rb.at[s - 1, j], b_s.at[j, s - 1], b_r.at[j, s - 1], at(lat, lon_at(s), tm)
            )
            for s in range(1, n_lon)
        ]

    peers = [(t, s) for s in range(n_lat - 1, -1, -1) for t in (1, 0) if (t, s) != (0, 0)]

    def peer(t, s):
        to = lax.rem(lat + s, n_lat)
        return (1 - upper if t else upper) * 4 + to, at(to, lon, cross if t else tm)

    def eighths(j):
        total = sb[j, :, lon].astype(F32)
        for s in range(1, n_lon):
            total = total + rb[s - 1, j].astype(F32)
        sc[j] = total.astype(BF16)
        home8[j] = sc[j, eighth].astype(F32)
        copies = []
        for i, (t, s) in enumerate(peers):
            place, where = peer(t, s)
            copies.append(remote(sc.at[j, place], rd.at[i, j], d_s.at[j, i], d_r.at[j, i], where))
        return copies

    def eighths_back(j):
        total = home8[j]
        for i in range(len(peers)):
            total = total + rd[i, j].astype(F32)
        fin[odd, j, eighth] = total.astype(BF16)
        own = fin.at[odd, j, eighth]
        return [
            remote(own, own, e_s.at[j, i], e_r.at[j, i], peer(t, s)[1]) for i, (t, s) in enumerate(peers)
        ]

    def pair_back(j):
        own = fin.at[odd, j]
        return [remote(own, own, g_s.at[j], g_r.at[j], at(lat, lon, pair))]

    def finish(j):
        for h in (0, 1):
            for tile in range(8):
                lane = (8 * j + tile) * 128
                if lane < half:
                    grad_ref[:, h * half + lane : h * half + lane + 128] = fin[h, j, tile]
        return []

    stages = [lon_stage, eighths, eighths_back, pair_back, finish]
    flying = {}
    for stage in stages:
        for j in range(chunks):
            for copy in flying.get(j, []):
                copy.wait()
            flying[j] = stage(j)
            for copy in flying[j]:
                copy.start()
    for turn in range(ITERS):
        for m in range(len(AROUND)):
            copy, sends, _ = adjoint(turn, m)
            pl.when(sends)(copy.wait_send)
    if aligned:
        for copy in [*gathers.values(), *relays.values()]:
            copy.wait_send()


def body(sizes, signal, dictionary, codes_init, thresholds):
    n_lat, n_lon, n_tm, atoms, rows, cols, half, padded = sizes
    channels = signal.shape[1]
    patch = channels * 16
    positions = rows * cols
    owned = dictionary.shape[0]
    target = signal[0].reshape(channels, rows, 4, cols, 4).transpose(1, 3, 0, 2, 4).reshape(positions, patch)
    target = jnp.pad(target, ((0, 0), (0, padded - patch)))
    start = codes_init[0].reshape(atoms, positions).T
    order = jnp.asarray(cell_order(), BF16)
    ext = (2, rows + 1, 8 + cols, atoms)
    dma = pltpu.SemaphoreType.DMA
    chunks, spans = padded // 256, -(-padded // 512)
    codes, grad = pl.pallas_call(
        functools.partial(kernel, sizes),
        out_shape=(
            jax.ShapeDtypeStruct((positions, atoms), F32),
            jax.ShapeDtypeStruct(dictionary.shape, BF16),
        ),
        in_specs=[pl.BlockSpec(memory_space=pltpu.VMEM)] * 5,
        out_specs=(pl.BlockSpec(memory_space=pltpu.VMEM),) * 2,
        scratch_shapes=[
            pltpu.VMEM((n_lon, 2, owned, half), BF16),
            pltpu.VMEM((8 * atoms, padded), BF16),
            pltpu.VMEM((8, 128) if owned % 16 == 0 else (8 * atoms, padded), F32),
            pltpu.VMEM((positions, 8 * atoms), F32),
            pltpu.VMEM((ITERS,) + ext, F32),
            pltpu.VMEM((ITERS, len(AROUND)) + ext, F32),
            pltpu.VMEM(ext, F32),
            pltpu.VMEM(ext, F32),
            pltpu.VMEM(ext, F32),
            pltpu.VMEM((2, positions, 4 * atoms), BF16),
            pltpu.VMEM((chunks, 4 * atoms, 256), F32),
            pltpu.VMEM((chunks, 4 * atoms, 256), F32),
            pltpu.VMEM((chunks, 4 * atoms, 256), F32),
            pltpu.VMEM((chunks, 8, n_lon, owned, 128), BF16),
            pltpu.VMEM((n_lon - 1, chunks, 8, owned, 128), BF16),
            pltpu.VMEM((chunks, 8, owned, 128), BF16),
            pltpu.VMEM((chunks, owned, 128), F32),
            pltpu.VMEM((7, chunks, owned, 128), BF16),
            pltpu.VMEM((2, chunks, 8, owned, 128), BF16),
            dma((spans, n_lon - 1)), dma((spans, n_lon - 1)), dma((spans, n_lon - 1)), dma((spans, n_lon - 1)),
            dma((8,)), dma((8,)), dma((ITERS, len(AROUND))), dma((ITERS, len(AROUND))),
            dma((chunks,)), dma((chunks,)), dma((chunks, n_lon - 1)), dma((chunks, n_lon - 1)),
            dma((chunks, 7)), dma((chunks, 7)), dma((chunks, 7)), dma((chunks, 7)),
            dma((chunks,)), dma((chunks,)),
        ],
        compiler_params=pltpu.CompilerParams(
            collective_id=0, has_side_effects=True, vmem_limit_bytes=48 * 2**20
        ),
        cost_estimate=pl.CostEstimate(flops=10**9, bytes_accessed=4 * 10**6, transcendentals=0),
    )(dictionary, order, target, start, thresholds[None, :])
    scale = 1.0 / math.sqrt(n_tm * n_lat * n_lon * positions)
    return codes.T.reshape(1, atoms, rows, cols), grad.astype(F32) * scale


def solution(mesh):
    n_lat, n_lon, n_tm = mesh.shape["lat"], mesh.shape["lon"], mesh.shape["tm"]
    assert n_lat == 4 and n_tm == 4 and n_lon >= 2
    placed = (P("tm", None, "lat", "lon"), P("lon", None), P("tm", None, "lat", "lon"), P())

    def part(signal, dictionary, codes_init, thresholds):
        atoms, rows, cols = codes_init.shape[1:]
        half = dictionary.shape[1] // 2
        sizes = (n_lat, n_lon, n_tm, atoms, rows, cols, half, -(-half // GROUP) * 128)
        return body(sizes, signal, dictionary, codes_init, thresholds)

    return jax.shard_map(
        part,
        mesh=mesh,
        in_specs=placed,
        out_specs=(P("tm", None, "lat", "lon"), P("lon", None)),
        check_vma=False,
    )
```

```python
import functools
import math

import jax
import jax.numpy as jnp
import numpy as np
from jax import lax
from jax.experimental import pallas as pl
from jax.experimental.pallas import tpu as pltpu
from jax.sharding import PartitionSpec as P

ITERS = 2
STEP_SIZE = 0.5
MESH = pl.DeviceIdType.MESH
F32, BF16 = jnp.float32, jnp.bfloat16
COMBOS = [(h, a, b) for h in (0, 1) for a in (0, 1) for b in (0, 1)]
AROUND = sorted(
    [(t, a, b) for t in (-1, 0, 1) for a in (-1, 0, 1) for b in (-1, 0, 1) if (t, a, b) != (0, 0, 0)],
    key=lambda e: abs(e[0]) + abs(e[1]) + abs(e[2]),
)
GROUP = 512


def cell_order():
    c, a, u, b, v = np.meshgrid(*[np.arange(n) for n in (8, 2, 4, 2, 4)], indexing="ij")
    source = ((((c * 2 + a) * 4 + u) * 2 + b) * 4 + v).ravel()
    target = ((((a * 2 + b) * 8 + c) * 4 + u) * 4 + v).ravel()
    order = np.zeros((GROUP, GROUP), np.float32)
    order[source, target] = 1.0
    return order


def contract(x, y, dx, dy):
    return lax.dot_general(x, y, (((dx,), (dy,)), ((), ())), preferred_element_type=F32)


def kernel(
    sizes, d_ref, p_ref, x_ref, z0_ref, th_ref, codes_ref, grad_ref,
    dfull, bhat, stage, zs, cbuf, qbuf, acc, moving, current,
    zh, away, ra, sb, rb, sc, home8, rd, fin,
    dict_s, dict_r, relay_s, relay_r, halo_s, halo_r, adj_s, adj_r,
    a_s, a_r, b_s, b_r, d_s, d_r, e_s, e_r, g_s, g_r,
):
    n_lat, n_lon, n_tm, atoms, rows, cols, half, padded = sizes
    owned = atoms // n_lon
    lat, lon, tm = lax.axis_index("lat"), lax.axis_index("lon"), lax.axis_index("tm")
    left = 8
    full = left + cols
    groups = padded // 128

    def at(la, lo, t):
        return (la, lo, t)

    def remote(src, dst, send, recv, where):
        return pltpu.make_async_remote_copy(
            src_ref=src, dst_ref=dst, send_sem=send, recv_sem=recv, device_id=where, device_id_type=MESH
        )

    def lon_at(step):
        return lax.rem(lon + step + n_lon, n_lon)

    current[...] = jnp.zeros_like(current)
    for p in range(rows):
        current[0, 1 + p, left:full, :] = z0_ref[p]

    barrier = pltpu.get_barrier_semaphore()
    count = n_lat * n_lon * n_tm
    mine = (lat * n_lon + lon) * n_tm + tm

    def greet(step, carry):
        other = lax.rem(mine + step, count)
        where = (other // (n_lon * n_tm), lax.rem(other // n_tm, n_lon), lax.rem(other, n_tm))
        pl.semaphore_signal(barrier, inc=1, device_id=where, device_id_type=MESH)
        return carry

    lax.fori_loop(1, count, greet, 0)
    pl.semaphore_wait(barrier, count - 1)

    odd = lax.rem(tm, 2)
    upper = tm // 2
    pair = tm + 1 - 2 * odd
    cross = tm + 2 - 4 * upper

    def region(ref, head, da, dl, sender):
        r = (pl.ds(rows if sender else 0, 1)) if da else pl.ds(1, rows)
        c = (pl.ds(full - 8 if sender else 0, 8)) if dl else pl.ds(left, cols)
        return ref.at[head + (r, c)]

    def halo(m):
        dt, da, dl = COMBOS[m]
        copy = remote(
            region(current, (0,), da, dl, True), region(current, (dt,), da, dl, False), halo_s.at[m], halo_r.at[m],
            at(lax.rem(lat + da, n_lat), lon_at(dl), lax.rem(tm + dt, n_tm)),
        )
        sends = (tm + dt < n_tm) & (lat + da < n_lat)
        gets = (tm - dt >= 0) & (lat - da >= 0)
        return copy, sends, gets

    def facing(et, ea, el, sender):
        h = pl.ds(0, 2) if et == 0 else pl.ds(1 if (et > 0) == sender else 0, 1)
        r = pl.ds(0, rows + 1) if ea == 0 else pl.ds(0 if (ea > 0) == sender else rows, 1)
        c = pl.ds(0, full) if el == 0 else pl.ds(0 if (el > 0) == sender else full - 8, 8)
        return h, r, c

    def inside(et, ea):
        return (tm + et >= 0) & (tm + et < n_tm) & (lat + ea >= 0) & (lat + ea < n_lat)

    def adjoint(turn, m):
        et, ea, el = AROUND[m]
        copy = remote(
            cbuf.at[(turn,) + facing(et, ea, el, True)], qbuf.at[(turn, m) + facing(et, ea, el, False)],
            adj_s.at[turn, m], adj_r.at[turn, m],
            at(lax.rem(lat - ea + n_lat, n_lat), lon_at(-el), lax.rem(tm - et + n_tm, n_tm)),
        )
        return copy, inside(-et, -ea), inside(et, ea)

    lanes = [(g, min(g + 4, groups)) for g in range(0, groups, 4)]
    spans = [(g0 * GROUP, min(g1 * GROUP, half)) for g0, g1 in lanes]
    gathers = {}
    for c, (first, last) in enumerate(spans):
        for s in range(1, n_lon):
            copy = remote(
                d_ref.at[:, pl.ds(pl.multiple_of(odd * half + first, 128), last - first)],
                dfull.at[lon, odd, :, pl.ds(first, last - first)],
                dict_s.at[c, s - 1], dict_r.at[c, s - 1], at(lat, lon_at(s), tm),
            )
            copy.start()
            gathers[c, s] = copy
        if c == 0:
            for m in range(1, 8):
                copy, sends, _ = halo(m)
                pl.when(sends)(copy.start)

    order = p_ref[...]

    def lay_out(load, place, chunk):
        g0, g1 = lanes[chunk]
        pieces = []
        for g in range(g0, g1):
            width = min(GROUP, half - g * GROUP)
            piece = load(g * GROUP, width)
            if width < GROUP:
                piece = jnp.concatenate([piece, jnp.zeros((owned, GROUP - width), BF16)], axis=1)
            pieces.append(piece)
        cells = jnp.dot(jnp.concatenate(pieces, axis=0), order, preferred_element_type=F32)
        for g in range(g0, g1):
            for ab in range(4):
                place(ab * atoms, g * 128, cells[(g - g0) * owned : (g - g0 + 1) * owned, ab * 128 : (ab + 1) * 128])

    aligned = owned % 16 == 0

    def place_at(owner, h):
        def place(row, lane, value):
            if aligned:
                start = pl.multiple_of(h * 4 * atoms + row + owner * owned, 16)
                bhat[pl.ds(start, owned), lane : lane + 128] = value.astype(BF16)
            else:
                start = h * 4 * atoms + row + owner * owned
                stage[start : start + owned, lane : lane + 128] = value
        return place

    def lay_out_small(owner, h, chunk):
        for g in range(*lanes[chunk]):
            width = min(GROUP, half - g * GROUP)
            cells = jnp.dot(held(owner, h)(g * GROUP, width), order[:width], preferred_element_type=F32)
            for ab in range(4):
                place_at(owner, h)(ab * atoms, g * 128, cells[:, ab * 128 : (ab + 1) * 128])

    def held(owner, h):
        return lambda lane, width: dfull[owner, h, :, lane : lane + width]

    if aligned:
        for c in range(len(lanes)):
            for h in (0, 1):
                lay_out(
                    lambda lane, width: d_ref[:, h * half + lane : h * half + lane + width], place_at(lon, h), c
                )
    relays = {}

    def relayed(c):
        for s in range(1, n_lon):
            source = lon_at(-s)
            relays[c, s].wait_recv()
            if aligned:
                lay_out(held(source, 1 - odd), place_at(source, 1 - odd), c)

    for c, (first, last) in enumerate(spans):
        for s in range(1, n_lon):
            source = lon_at(-s)
            gathers[c, s].wait_recv()
            part = dfull.at[source, odd, :, pl.ds(first, last - first)]
            copy = remote(part, part, relay_s.at[c, s - 1], relay_r.at[c, s - 1], at(lat, lon, pair))
            copy.start()
            relays[c, s] = copy
            if aligned:
                lay_out(held(source, odd), place_at(source, odd), c)
        if c > 0:
            relayed(c - 1)
    relayed(len(lanes) - 1)
    if not aligned:
        for copy in [*gathers.values(), *relays.values()]:
            copy.wait_send()
        for h in (0, 1):
            dfull[lon, h] = d_ref[:, h * half : (h + 1) * half]
            for c in range(len(lanes)):
                for owner in range(n_lon):
                    lay_out_small(owner, h, c)
        bhat[...] = stage[...].astype(BF16)

    def stack_codes(held):
        for i, (h, a, b) in enumerate(COMBOS):
            for p in range(rows):
                zs[p * cols : (p + 1) * cols, i * atoms : (i + 1) * atoms] = held[
                    h, 1 + p - a, left - b : full - b, :
                ]
        return zs[...].astype(BF16)

    def residual(stacked):
        synth = jnp.dot(stacked, bhat[...], preferred_element_type=F32)
        return (synth - x_ref[...].astype(F32)).astype(BF16)

    shrink = STEP_SIZE * th_ref[...]
    momentum = 1.0
    first_hour = jnp.where(tm > 0, 1.0, 0.0)
    first_band = jnp.where(lat > 0, 1.0, 0.0)
    for m in range(1, 8):
        copy, sends, gets = halo(m)
        pl.when(gets)(copy.wait_recv)
        pl.when(sends)(copy.wait_send)
    moving[...] = current[...]
    for turn in range(ITERS):
        resid = residual(stack_codes(moving))
        terms = contract(resid, bhat[...], 1, 1)
        cbuf[turn] = jnp.zeros_like(cbuf[turn])
        for i, (h, a, b) in enumerate(COMBOS):
            for p in range(rows):
                cbuf[turn, h, 1 + p - a, left - b : full - b, :] += terms[
                    p * cols : (p + 1) * cols, i * atoms : (i + 1) * atoms
                ]
        for m in reversed(range(len(AROUND))):
            copy, sends, _ = adjoint(turn, m)
            pl.when(sends)(copy.start)
        acc[...] = cbuf[turn]
        for m in range(len(AROUND)):
            copy, _, gets = adjoint(turn, m)

            def add(copy=copy, m=m):
                copy.wait_recv()
                h, r, c = facing(*AROUND[m], False)
                acc[h, r, c, :] += qbuf[turn, m, h, r, c, :]

            pl.when(gets)(add)
        later = (1.0 + math.sqrt(1.0 + 4.0 * momentum * momentum)) / 2.0
        weight = (momentum - 1.0) / later
        momentum = later
        for h in (0, 1):
            for r in range(rows + 1):
                descent = moving[h, r] - STEP_SIZE * acc[h, r]
                updated = jnp.where(
                    descent > shrink, descent - shrink, jnp.where(descent < -shrink, descent + shrink, 0.0)
                )
                if h:
                    updated = updated * first_hour
                if r == 0:
                    updated = updated * first_band
                moving[h, r] = updated + weight * (updated - current[h, r])
                current[h, r] = updated
    for p in range(rows):
        codes_ref[p] = current[0, 1 + p, left:full, :]
    stacked = stack_codes(current)
    resid = residual(stacked)

    wide = 4 * atoms
    chunks = groups // 2
    for h in (0, 1):
        zh[h] = stacked[:, h * wide : (h + 1) * wide]
    part_of = [resid[:, j * 256 : (j + 1) * 256] for j in range(chunks)]
    pairs = []
    for j in range(chunks):
        away[j] = contract(zh[1 - odd], part_of[j], 0, 0)
        copy = remote(away.at[j], ra.at[j], a_s.at[j], a_r.at[j], at(lat, lon, pair))
        copy.start()
        pairs.append(copy)
    eighth = upper * 4 + lat

    def lon_stage(j):
        own = contract(zh[odd], part_of[j], 0, 0)
        pairs[j].wait()
        part = (own + ra[j]).astype(BF16)
        cells = jnp.concatenate(
            [
                jnp.concatenate(
                    [part[ab * atoms : (ab + 1) * atoms, g * 128 : (g + 1) * 128] for ab in range(4)], axis=1
                )
                for g in (0, 1)
            ],
            axis=0,
        )
        plain = contract(cells, order, 1, 1)
        for tile in range(8):
            row, lane = tile // 4 * atoms, tile % 4 * 128
            for owner in range(n_lon):
                sb[j, tile, owner] = plain[
                    row + owner * owned : row + (owner + 1) * owned, lane : lane + 128
                ].astype(BF16)
        return [
            remote(
                sb.at[j, :, lon_at(s)], rb.at[s - 1, j], b_s.at[j, s - 1], b_r.at[j, s - 1], at(lat, lon_at(s), tm)
            )
            for s in range(1, n_lon)
        ]

    peers = [(t, s) for s in range(n_lat - 1, -1, -1) for t in (1, 0) if (t, s) != (0, 0)]

    def peer(t, s):
        to = lax.rem(lat + s, n_lat)
        return (1 - upper if t else upper) * 4 + to, at(to, lon, cross if t else tm)

    def eighths(j):
        total = sb[j, :, lon].astype(F32)
        for s in range(1, n_lon):
            total = total + rb[s - 1, j].astype(F32)
        sc[j] = total.astype(BF16)
        home8[j] = sc[j, eighth].astype(F32)
        copies = []
        for i, (t, s) in enumerate(peers):
            place, where = peer(t, s)
            copies.append(remote(sc.at[j, place], rd.at[i, j], d_s.at[j, i], d_r.at[j, i], where))
        return copies

    def eighths_back(j):
        total = home8[j]
        for i in range(len(peers)):
            total = total + rd[i, j].astype(F32)
        fin[odd, j, eighth] = total.astype(BF16)
        own = fin.at[odd, j, eighth]
        return [
            remote(own, own, e_s.at[j, i], e_r.at[j, i], peer(t, s)[1]) for i, (t, s) in enumerate(peers)
        ]

    def pair_back(j):
        own = fin.at[odd, j]
        return [remote(own, own, g_s.at[j], g_r.at[j], at(lat, lon, pair))]

    def finish(j):
        for h in (0, 1):
            for tile in range(8):
                lane = (8 * j + tile) * 128
                if lane < half:
                    grad_ref[:, h * half + lane : h * half + lane + 128] = fin[h, j, tile]
        return []

    stages = [lon_stage, eighths, eighths_back, pair_back, finish]
    flying = {}
    for stage in stages:
        for j in range(chunks):
            for copy in flying.get(j, []):
                copy.wait()
            flying[j] = stage(j)
            for copy in flying[j]:
                copy.start()
    for turn in range(ITERS):
        for m in range(len(AROUND)):
            copy, sends, _ = adjoint(turn, m)
            pl.when(sends)(copy.wait_send)
    if aligned:
        for copy in [*gathers.values(), *relays.values()]:
            copy.wait_send()


def body(sizes, signal, dictionary, codes_init, thresholds):
    n_lat, n_lon, n_tm, atoms, rows, cols, half, padded = sizes
    channels = signal.shape[1]
    patch = channels * 16
    positions = rows * cols
    owned = dictionary.shape[0]
    target = signal[0].reshape(channels, rows, 4, cols, 4).transpose(1, 3, 0, 2, 4).reshape(positions, patch)
    target = jnp.pad(target, ((0, 0), (0, padded - patch)))
    start = codes_init[0].transpose(1, 2, 0)
    order = jnp.asarray(cell_order(), BF16)
    ext = (2, rows + 1, 8 + cols, atoms)
    dma = pltpu.SemaphoreType.DMA
    chunks, spans = padded // 256, -(-padded // 512)
    codes, grad = pl.pallas_call(
        functools.partial(kernel, sizes),
        out_shape=(
            jax.ShapeDtypeStruct((rows, cols, atoms), F32),
            jax.ShapeDtypeStruct(dictionary.shape, BF16),
        ),
        in_specs=[pl.BlockSpec(memory_space=pltpu.VMEM)] * 5,
        out_specs=(pl.BlockSpec(memory_space=pltpu.VMEM),) * 2,
        scratch_shapes=[
            pltpu.VMEM((n_lon, 2, owned, half), BF16),
            pltpu.VMEM((8 * atoms, padded), BF16),
            pltpu.VMEM((8, 128) if owned % 16 == 0 else (8 * atoms, padded), F32),
            pltpu.VMEM((positions, 8 * atoms), F32),
            pltpu.VMEM((ITERS,) + ext, F32),
            pltpu.VMEM((ITERS, len(AROUND)) + ext, F32),
            pltpu.VMEM(ext, F32),
            pltpu.VMEM(ext, F32),
            pltpu.VMEM(ext, F32),
            pltpu.VMEM((2, positions, 4 * atoms), BF16),
            pltpu.VMEM((chunks, 4 * atoms, 256), F32),
            pltpu.VMEM((chunks, 4 * atoms, 256), F32),
            pltpu.VMEM((chunks, 8, n_lon, owned, 128), BF16),
            pltpu.VMEM((n_lon - 1, chunks, 8, owned, 128), BF16),
            pltpu.VMEM((chunks, 8, owned, 128), BF16),
            pltpu.VMEM((chunks, owned, 128), F32),
            pltpu.VMEM((7, chunks, owned, 128), BF16),
            pltpu.VMEM((2, chunks, 8, owned, 128), BF16),
            dma((spans, n_lon - 1)), dma((spans, n_lon - 1)), dma((spans, n_lon - 1)), dma((spans, n_lon - 1)),
            dma((8,)), dma((8,)), dma((ITERS, len(AROUND))), dma((ITERS, len(AROUND))),
            dma((chunks,)), dma((chunks,)), dma((chunks, n_lon - 1)), dma((chunks, n_lon - 1)),
            dma((chunks, 7)), dma((chunks, 7)), dma((chunks, 7)), dma((chunks, 7)),
            dma((chunks,)), dma((chunks,)),
        ],
        compiler_params=pltpu.CompilerParams(
            collective_id=0, has_side_effects=True, vmem_limit_bytes=48 * 2**20
        ),
        cost_estimate=pl.CostEstimate(flops=10**9, bytes_accessed=4 * 10**6, transcendentals=0),
    )(dictionary, order, target, start, thresholds[None, :])
    scale = 1.0 / math.sqrt(n_tm * n_lat * n_lon * positions)
    return codes.transpose(2, 0, 1)[None], grad.astype(F32) * scale


def solution(mesh):
    n_lat, n_lon, n_tm = mesh.shape["lat"], mesh.shape["lon"], mesh.shape["tm"]
    assert n_lat == 4 and n_tm == 4 and n_lon >= 2
    placed = (P("tm", None, "lat", "lon"), P("lon", None), P("tm", None, "lat", "lon"), P())

    def part(signal, dictionary, codes_init, thresholds):
        atoms, rows, cols = codes_init.shape[1:]
        half = dictionary.shape[1] // 2
        sizes = (n_lat, n_lon, n_tm, atoms, rows, cols, half, -(-half // GROUP) * 128)
        return body(sizes, signal, dictionary, codes_init, thresholds)

    return jax.shard_map(
        part,
        mesh=mesh,
        in_specs=placed,
        out_specs=(P("tm", None, "lat", "lon"), P("lon", None)),
        check_vma=False,
    )
```
